32 devices in a mesh: wide: 8 (over z, x), narrow: 4 (over y, core).
Axes of the slice: x: 2, y: 2, z: 4, core: 2. Of those that a mesh axis runs over, the one named last changes fastest.
Arguments:
- latent: bfloat16 [8, 32, 48, 256], P('wide', 'narrow'), may hold values from -12 to 12
- conv_first: bfloat16 [6912, 256], P(None, 'wide'), may hold values from -0.078125 to 0.078125
- conv_second: bfloat16 [6912, 256], P(None, 'wide'), may hold values from -0.078125 to 0.078125
- embed_weight: bfloat16 [1024, 2240], P(None, 'wide'), may hold values from -0.1875 to 0.1875
- qkv_weight: bfloat16 [3, 2240, 2240], P(None, None, 'narrow'), may hold values from -0.125 to 0.125
Outputs:
- mixed: bfloat16 [3072, 2240], P('wide', 'narrow')
The draws below stay inside these ranges and needn't reach their ends.
All inputs are finite; a program needn't handle non-finite values.
Results may differ from the reference program's by a relative error of at most 0.011.
Values may be sent and summed in bfloat16 or wider, within the bound.
A program may use at most 128 MiB of HBM per device.

```python
import jax
import jax.numpy as jnp
from jax import lax

C = 256
HEADS = 20
HEAD_DIM = 112
LAT_W = 48
D = 2240
H = 32
FRAMES = 8


def draw_latent(key, part):
    noise_key, common_key, frame_key = jax.random.split(jax.random.fold_in(key, 17), 3)
    full_shape = (FRAMES, H, LAT_W, C)
    noise_part = jax.random.normal(noise_key, full_shape, jnp.float32)
    common = jax.random.normal(common_key, (1, 1, 1, C), jnp.float32)
    per_frame = 0.7 * jax.random.normal(frame_key, (FRAMES, 1, 1, C), jnp.float32)
    return jnp.clip(noise_part + common + per_frame, -12.0, 12.0).astype(jnp.bfloat16)


def block_levels(own_key, dims, cuts, smallest, high):
    def one(position, parts):
        steps = jax.random.uniform(jax.random.fold_in(jax.random.fold_in(own_key, 6), position), (parts,), jnp.float32, smallest / len(cuts), high / len(cuts))
        return jnp.repeat(jnp.exp(steps), dims[position] // parts).reshape((-1,) + (1,) * (len(dims) - position - 1))

    level = one(*cuts[0])
    for cut in cuts[1:]:
        level = level * one(*cut)
    return level


def scatter_about(stream_key, extent, scale, reach, cuts=(), dtype=jnp.bfloat16):
    array = scale * jax.random.normal(stream_key, extent, jnp.float32)
    if cuts:
        array = array * block_levels(stream_key, extent, cuts, -0.22, 0.18)
    return jnp.clip(array, -reach, reach).astype(dtype)


def setup_inputs(seed: int = 0) -> dict:
    keys = jax.random.split(jax.random.key(seed), 6)
    latent = draw_latent(jax.random.fold_in(keys[5], 71), 0)
    conv_first = scatter_about(keys[1], (27 * C, C), (27 * C) ** -0.5, 0.078125, ((1, 8),))
    conv_second = scatter_about(keys[2], (27 * C, C), (27 * C) ** -0.5, 0.078125, ((1, 8),))
    embed_weight = scatter_about(keys[3], (4 * C, D), (4 * C) ** -0.5, 0.1875, ((1, 8),))
    qkv_weight = scatter_about(keys[4], (3, D, D), D ** -0.5, 0.125, ((2, 4),))
    return {"latent": latent, "conv_first": conv_first, "conv_second": conv_second, "embed_weight": embed_weight, "qkv_weight": qkv_weight}


def causal_conv(volume, weight):
    frame_count, row_count, col_count, chan_count = volume.shape
    padded = jnp.pad(volume, ((2, 0), (1, 1), (1, 1), (0, 0)))
    summed = jnp.zeros((frame_count * row_count * col_count, weight.shape[1]), jnp.float32)
    for kernel_tap in range(27):
        time_step = kernel_tap // 9
        row_step = (kernel_tap // 3) % 3
        col_step = kernel_tap % 3
        window = padded[time_step:time_step + frame_count, row_step:row_step + row_count, col_step:col_step + col_count]
        window = window.reshape(-1, chan_count)
        summed = summed + jnp.dot(window, weight[kernel_tap * chan_count:(kernel_tap + 1) * chan_count], preferred_element_type=jnp.float32)
    return summed


def frame_step(carry, inputs):
    state, key_total = carry
    query_feat, key_feat, val_rows = inputs
    token_count = query_feat.shape[0]
    query_wide = query_feat.astype(jnp.float32)
    key_wide = key_feat.astype(jnp.float32)
    val_wide = val_rows.astype(jnp.float32)
    scores = jnp.einsum("thd,shd->hts", query_wide, key_wide, precision=lax.Precision.HIGHEST)
    order_ids = jnp.arange(token_count)
    allowed = order_ids[None, :] <= order_ids[:, None]
    scores = jnp.where(allowed[None], scores, 0.0)
    local_den = jnp.sum(scores, axis=-1)
    weight_low = scores.astype(jnp.bfloat16).astype(jnp.float32)
    local_num = jnp.einsum("hts,she->the", weight_low, val_wide, precision=lax.Precision.HIGHEST)
    carried_num = jnp.einsum("thd,hde->the", query_wide, state, precision=lax.Precision.HIGHEST)
    carried_den = jnp.einsum("thd,hd->th", query_wide, key_total, precision=lax.Precision.HIGHEST)
    result = (local_num + carried_num) / (local_den.T + carried_den)[..., None]
    new_state = state + jnp.einsum("thd,the->hde", key_wide, val_wide, precision=lax.Precision.HIGHEST)
    new_total = key_total + jnp.sum(key_wide, axis=0)
    return (new_state, new_total), result.astype(jnp.bfloat16).reshape(token_count, -1)


def reference(latent, conv_first, conv_second, embed_weight, qkv_weight):
    frame_count, row_count, col_count, chan_count = latent.shape
    first = causal_conv(latent, conv_first)
    activated = jax.nn.silu(first).astype(jnp.bfloat16).reshape(latent.shape)
    second = causal_conv(activated, conv_second) + latent.reshape(-1, chan_count).astype(jnp.float32)
    block_out = second.astype(jnp.bfloat16)
    patches = block_out.reshape(frame_count, row_count // 2, 2, col_count // 2, 2, chan_count)
    patches = patches.transpose(0, 1, 3, 2, 4, 5).reshape(-1, 4 * chan_count)
    embedded = jnp.dot(patches, embed_weight, preferred_element_type=jnp.float32).astype(jnp.bfloat16)
    projected = [jnp.dot(embedded, qkv_weight[which_part], preferred_element_type=jnp.float32).astype(jnp.bfloat16) for which_part in range(3)]
    query_feat = (jax.nn.elu(projected[0].astype(jnp.float32)) + 1.0).astype(jnp.bfloat16)
    key_feat = (jax.nn.elu(projected[1].astype(jnp.float32)) + 1.0).astype(jnp.bfloat16)
    head_shape = (frame_count, -1, HEADS, HEAD_DIM)
    initial = (jnp.zeros((HEADS, HEAD_DIM, HEAD_DIM), jnp.float32), jnp.zeros((HEADS, HEAD_DIM), jnp.float32))
    final_carry, mixed = lax.scan(frame_step, initial, (query_feat.reshape(head_shape), key_feat.reshape(head_shape), projected[2].reshape(head_shape)))
    return mixed.reshape(-1, HEADS * HEAD_DIM)
```

```python
import functools

import jax
import jax.numpy as jnp
from jax import lax
from jax.experimental import pallas as pl
from jax.experimental.pallas import tpu as pltpu
from jax.sharding import PartitionSpec as P

HEAD_DIM = 112
LANE = 128
MESH = pl.DeviceIdType.MESH


def strips(lanes):
    half = lanes // LANE // 2
    return half, max(1, half // 3)


def gather_kernel(wide, narrow, shapes, *refs):
    count = len(shapes)
    mine, full = refs[:count], refs[count : 2 * count]
    own_sem, send_sem, recv_sem = refs[2 * count :]
    w = lax.axis_index("wide")
    n = lax.axis_index("narrow")
    z, x = w // 2, lax.rem(w, 2)
    y, core = lax.rem(n // 2, 2), lax.rem(n, 2)
    depth = wide // 2
    peer_x = {"wide": w + 1 - 2 * x}
    peer_y = {"narrow": n + 2 - 4 * y}
    peer_core = {"narrow": n + 1 - 2 * core}
    above, below = {"wide": w + 2}, {"wide": w - 2}
    has_above, has_below = z < depth - 1, z > 0

    barrier = pltpu.get_barrier_semaphore()
    for peer in (peer_x, peer_y, peer_core):
        pl.semaphore_signal(barrier, inc=1, device_id=peer, device_id_type=MESH)

    @pl.when(has_above)
    def _():
        pl.semaphore_signal(barrier, inc=1, device_id=above, device_id_type=MESH)

    @pl.when(has_below)
    def _():
        pl.semaphore_signal(barrier, inc=1, device_id=below, device_id_type=MESH)

    pl.semaphore_wait(barrier, 3 + has_above.astype(jnp.int32) + has_below.astype(jnp.int32))

    def window(part, shard, kind):
        half, third = strips(shapes[part][1])
        start, size = {
            "own": (core * half + y * third, half - third),
            "to_y": (core * half + y * (half - third), third),
            "from_y": (core * half + (1 - y) * (half - third), third),
            "core_own": ((1 - core) * half + y * third, half - third),
            "core_y": ((1 - core) * half + (1 - y) * (half - third), third),
        }[kind]
        cols = pl.ds(pl.multiple_of(start * LANE, LANE), size * LANE)
        return (shard, slice(None), cols)

    def transfer(part, shard, kind, lane, peer, own=False):
        at = window(part, shard, kind)
        target = full[part].at[at]
        source = mine[part].at[at[1:]] if own else target
        arrive = {"own": 0, "to_y": 1, "from_y": 3}[kind]
        if lane == "core" and kind == "own":
            arrive = 2
        send = ("up", "down", "x", "y", "core", "core_y").index(lane if kind != "from_y" else "core_y")
        return pltpu.make_async_remote_copy(
            src_ref=source,
            dst_ref=target,
            send_sem=send_sem.at[part, shard, send],
            recv_sem=recv_sem.at[part, shard, arrive],
            device_id=peer,
            device_id_type=MESH,
        )

    def landed(part, shard, kind):
        at = window(part, shard, kind)
        target = full[part].at[at]
        arrive = {"own": 0, "from_y": 1, "core_own": 2, "core_y": 3}[kind]
        return pltpu.make_async_remote_copy(
            src_ref=target,
            dst_ref=target,
            send_sem=send_sem.at[part, shard, 0],
            recv_sem=recv_sem.at[part, shard, arrive],
            device_id=peer_core,
            device_id_type=MESH,
        )

    def pass_on(part, shard):
        transfer(part, shard, "to_y", "y", peer_y).start()
        transfer(part, shard, "own", "core", peer_core).start()

    def from_partner(part, row):
        shard = 2 * row + 1 - x
        landed(part, shard, "own").wait_recv()
        pass_on(part, shard)

    def from_y(part, shard):
        landed(part, shard, "from_y").wait_recv()
        transfer(part, shard, "from_y", "core", peer_core).start()

    def stage(part, d):
        if d == 0:
            @pl.when(has_above)
            def _():
                transfer(part, w, "own", "up", above, own=True).start()

            @pl.when(has_below)
            def _():
                transfer(part, w, "own", "down", below, own=True).start()

            transfer(part, w, "own", "x", peer_x, own=True).start()
            pltpu.make_async_copy(mine[part], full[part].at[w], own_sem.at[part]).start()
            return

        @pl.when(z >= d)
        def _():
            shard = w - 2 * d
            landed(part, shard, "own").wait_recv()

            @pl.when(has_above)
            def _():
                transfer(part, shard, "own", "up", above).start()

            transfer(part, shard, "own", "x", peer_x).start()
            pass_on(part, shard)

        @pl.when(z + d < depth)
        def _():
            shard = w + 2 * d
            landed(part, shard, "own").wait_recv()

            @pl.when(has_below)
            def _():
                transfer(part, shard, "own", "down", below).start()

            transfer(part, shard, "own", "x", peer_x).start()
            pass_on(part, shard)

        late(part, d - 1)

    def late(part, d):
        for sign in (-1, 1) if d else (1,):
            row = z + sign * d

            @pl.when((row >= 0) & (row < depth))
            def _():
                from_partner(part, row)
        if d >= 1:
            later(part, d - 1)

    def later(part, d):
        for sign in (-1, 1) if d else (1,):
            row = z + sign * d

            @pl.when((row >= 0) & (row < depth))
            def _():
                if d:
                    from_y(part, 2 * row + x)
                from_y(part, 2 * row + 1 - x)

    for tick in range(count + depth + 1):
        for part in range(count):
            d = tick - part
            if 0 <= d < depth:
                stage(part, d)
            elif d == depth:
                late(part, d - 1)
            elif d == depth + 1:
                later(part, d - 2 + 0)

    for part in range(count):
        pltpu.make_async_copy(mine[part], full[part].at[w], own_sem.at[part]).wait()
        for row in range(depth):
            for side in range(2):
                shard = 2 * row + side

                @pl.when(shard != w)
                def _():
                    landed(part, shard, "core_own").wait_recv()
                    landed(part, shard, "core_y").wait_recv()
                    transfer(part, shard, "to_y", "y", peer_y).wait_send()
                    transfer(part, shard, "own", "core", peer_core).wait_send()
                    transfer(part, shard, "from_y", "core", peer_core).wait_send()

                @pl.when(side == x)
                def _():
                    transfer(part, shard, "own", "x", peer_x).wait_send()

                    @pl.when(has_above & (row <= z))
                    def _():
                        transfer(part, shard, "own", "up", above).wait_send()

                    @pl.when(has_below & (row >= z))
                    def _():
                        transfer(part, shard, "own", "down", below).wait_send()


def gather_weights(parts):
    wide, narrow = lax.axis_size("wide"), lax.axis_size("narrow")
    shapes = [part.shape for part in parts]
    count = len(parts)
    return pl.pallas_call(
        functools.partial(gather_kernel, wide, narrow, shapes),
        out_shape=[jax.ShapeDtypeStruct((wide,) + shape, jnp.bfloat16) for shape in shapes],
        in_specs=[pl.BlockSpec(memory_space=pl.ANY)] * count,
        out_specs=[pl.BlockSpec(memory_space=pl.ANY)] * count,
        scratch_shapes=[
            pltpu.SemaphoreType.DMA((count,)),
            pltpu.SemaphoreType.DMA((count, wide, 6)),
            pltpu.SemaphoreType.DMA((count, wide, 4)),
        ],
        compiler_params=pltpu.CompilerParams(collective_id=0, has_side_effects=True),
    )(*parts)


def shifted(x, axis, by):
    size = lax.axis_size(axis)
    pairs = [(i, i + by) for i in range(size) if 0 <= i + by < size]
    return lax.ppermute(x, axis, pairs)


def extended(block, sides, width):
    for axis, dim in sides:
        count = lax.axis_size(axis)
        forward = [(i, i + 1) for i in range(count - 1)]
        backward = [(target, source) for source, target in forward]
        low = lax.ppermute(
            lax.slice_in_dim(block, block.shape[dim] - width, None, axis=dim), axis, forward
        )
        high = lax.ppermute(lax.slice_in_dim(block, 0, width, axis=dim), axis, backward)
        block = jnp.concatenate([low, block, high], axis=dim)
    return block


def causal_conv(current, weight):
    before = shifted(current, "wide", 1)
    earlier = shifted(current, "wide", 2)
    stacked = jnp.concatenate([earlier, before, current], axis=0)
    rimmed = extended(stacked, (("narrow", 1),), 1)
    padded = jnp.pad(rimmed, ((0, 0), (0, 0), (1, 1), (0, 0)))
    row_count = current.shape[1]
    col_count = current.shape[2]
    chan_count = current.shape[3]
    summed = jnp.zeros((row_count * col_count, weight.shape[0]), jnp.float32)
    for kernel_tap in range(27):
        time_step = kernel_tap // 9
        row_step = kernel_tap // 3 % 3
        col_step = kernel_tap % 3
        window = padded[time_step, row_step : row_step + row_count, col_step : col_step + col_count]
        window = window.reshape(row_count * col_count, chan_count)
        summed = summed + lax.dot_general(
            window,
            weight[:, kernel_tap * chan_count : (kernel_tap + 1) * chan_count],
            (((1,), (1,)), ((), ())),
            preferred_element_type=jnp.float32,
        )
    return summed


def embed_tokens(patch_feats, embed_weight):
    return lax.dot_general(
        patch_feats,
        embed_weight,
        (((1,), (1,)), ((), ())),
        preferred_element_type=jnp.float32,
    ).astype(jnp.bfloat16)


def per_device(latent, conv_first, conv_second, embed_weight, qkv_weight):
    row_count = latent.shape[1]
    col_count = latent.shape[2]
    chan_count = latent.shape[3]
    conv_first, conv_second, embed_weight = (
        part.reshape(-1, part.shape[2])
        for part in gather_weights([conv_first.T, conv_second.T, embed_weight.T])
    )
    first = causal_conv(latent, conv_first)
    activated = jax.nn.silu(first).astype(jnp.bfloat16).reshape(latent.shape)
    second = causal_conv(activated, conv_second) + latent.reshape(-1, chan_count).astype(
        jnp.float32
    )
    block_out = second.astype(jnp.bfloat16)
    patches = block_out.reshape(row_count // 2, 2, col_count // 2, 2, chan_count)
    patches = patches.transpose(0, 2, 1, 3, 4).reshape(-1, 4 * chan_count)
    embedded = lax.all_gather(embed_tokens(patches, embed_weight), "narrow", axis=0, tiled=True)
    heads_here = qkv_weight.shape[2] // HEAD_DIM
    token_count = embedded.shape[0]
    query_raw = jnp.dot(embedded, qkv_weight[0], preferred_element_type=jnp.float32)
    key_raw = jnp.dot(embedded, qkv_weight[1], preferred_element_type=jnp.float32)
    val_rows = jnp.dot(embedded, qkv_weight[2], preferred_element_type=jnp.float32).astype(
        jnp.bfloat16
    )
    query_feat = (
        (jax.nn.elu(query_raw) + 1.0)
        .astype(jnp.bfloat16)
        .reshape(token_count, heads_here, HEAD_DIM)
    )
    key_feat = (
        (jax.nn.elu(key_raw) + 1.0).astype(jnp.bfloat16).reshape(token_count, heads_here, HEAD_DIM)
    )
    val_heads = val_rows.reshape(token_count, heads_here, HEAD_DIM)
    scores = jnp.einsum("thd,shd->hts", query_feat, key_feat, preferred_element_type=jnp.float32)
    row_ids = lax.broadcasted_iota(jnp.int32, (token_count, token_count), 0)
    col_ids = lax.broadcasted_iota(jnp.int32, (token_count, token_count), 1)
    scores = jnp.where((col_ids <= row_ids)[None], scores, 0.0)
    local_den = jnp.sum(scores, axis=-1)
    local_num = jnp.einsum(
        "hts,she->the", scores.astype(jnp.bfloat16), val_heads, preferred_element_type=jnp.float32
    )
    state_local = jnp.einsum(
        "thd,the->hde", key_feat, val_heads, preferred_element_type=jnp.float32
    )
    key_local = jnp.sum(key_feat, axis=0, dtype=jnp.float32)
    flat_state = jnp.concatenate([state_local.reshape(-1), key_local.reshape(-1)])
    length_all = flat_state.shape[0]
    peer_count = lax.axis_size("wide")
    per_peer = -(-length_all // peer_count)
    piece_grid = jnp.pad(flat_state, (0, per_peer * peer_count - length_all)).reshape(
        peer_count, per_peer
    )
    lower_ones = (
        lax.broadcasted_iota(jnp.int32, (peer_count, peer_count), 1)
        < lax.broadcasted_iota(jnp.int32, (peer_count, peer_count), 0)
    ).astype(jnp.float32)
    partial_sums = jnp.dot(
        lower_ones,
        lax.all_to_all(
            piece_grid.astype(jnp.bfloat16), "wide", split_axis=0, concat_axis=0, tiled=True
        ).astype(piece_grid.dtype),
        precision=lax.Precision.HIGHEST,
    )
    spread = lax.all_to_all(
        partial_sums.astype(jnp.bfloat16), "wide", split_axis=0, concat_axis=0, tiled=True
    ).astype(partial_sums.dtype)
    flat_prefix = spread.reshape(-1)[:length_all]
    state_size = state_local.size
    state_prev = flat_prefix[:state_size].reshape(state_local.shape)
    key_prev = flat_prefix[state_size:].reshape(key_local.shape)
    query_wide = query_feat.astype(jnp.float32)
    carried_num = jnp.einsum(
        "thd,hde->the", query_wide, state_prev, precision=lax.Precision.HIGHEST
    )
    carried_den = jnp.einsum("thd,hd->th", query_wide, key_prev, precision=lax.Precision.HIGHEST)
    result = (local_num + carried_num) / (local_den.T + carried_den)[..., None]
    return result.astype(jnp.bfloat16).reshape(token_count, heads_here * HEAD_DIM)


def solution(mesh):
    return jax.shard_map(
        per_device,
        mesh=mesh,
        in_specs=(
            P("wide", "narrow", None, None),
            P(None, "wide"),
            P(None, "wide"),
            P(None, "wide"),
            P(None, None, "narrow"),
        ),
        out_specs=P("wide", "narrow"),
        check_vma=False,
    )
```

```python
import functools

import jax
import jax.numpy as jnp
from jax import lax
from jax.experimental import pallas as pl
from jax.experimental.pallas import tpu as pltpu
from jax.sharding import PartitionSpec as P

HEAD_DIM = 112
LANE = 128
MESH = pl.DeviceIdType.MESH


def strips(lanes):
    half = lanes // LANE // 2
    return half, max(1, half // 3)


def block_kernel(
    wide, narrow, shapes, latent, first_w, second_w, embed_w, patches, embed_full,
    first_full, second_full, frames, halo_out, columns, total, lanes, own_sem, send_sem, recv_sem,
    edge_send, edge_recv, strip_send, strip_recv,
):
    count = len(shapes)
    mine = (first_w, second_w, embed_w)
    full = (first_full, second_full, embed_full)
    rows, cols, chans = latent.shape[1:]
    frames[...] = jnp.zeros_like(frames)
    halo_out[...] = jnp.zeros_like(halo_out)
    frames[2, 1 : rows + 1] = latent[0]
    w = lax.axis_index("wide")
    n = lax.axis_index("narrow")
    z, x = w // 2, lax.rem(w, 2)
    y, core = lax.rem(n // 2, 2), lax.rem(n, 2)
    depth = wide // 2
    peer_x = {"wide": w + 1 - 2 * x}
    peer_y = {"narrow": n + 2 - 4 * y}
    peer_core = {"narrow": n + 1 - 2 * core}
    above, below = {"wide": w + 2}, {"wide": w - 2}
    has_above, has_below = z < depth - 1, z > 0

    barrier = pltpu.get_barrier_semaphore()
    for peer in (peer_x, peer_y, peer_core):
        pl.semaphore_signal(barrier, inc=1, device_id=peer, device_id_type=MESH)

    @pl.when(has_above)
    def _():
        pl.semaphore_signal(barrier, inc=1, device_id=above, device_id_type=MESH)

    @pl.when(has_below)
    def _():
        pl.semaphore_signal(barrier, inc=1, device_id=below, device_id_type=MESH)

    def inside(frame, strip):
        return (frame >= 0) & (frame < wide) & (strip >= 0) & (strip < narrow)

    edges = [(j, i) for j in (2, 1, 0) for i in (0, -1, 1) if (j, i) != (0, 0)]
    expected = 3 + has_above.astype(jnp.int32) + has_below.astype(jnp.int32)
    for j, i in edges:
        @pl.when(inside(w - j, n - i))
        def _():
            pl.semaphore_signal(
                barrier, inc=1, device_id={"wide": w - j, "narrow": n - i}, device_id_type=MESH
            )

        expected = expected + inside(w + j, n + i).astype(jnp.int32)
    pl.semaphore_wait(barrier, expected)

    def edge_copy(which, index, toward=1):
        j, i = edges[index]
        ref = (frames, halo_out)[which]
        if i == 0:
            source, target = pl.ds(1, rows), pl.ds(1, rows)
        elif i == 1:
            source, target = pl.ds(rows, 1), pl.ds(0, 1)
        else:
            source, target = pl.ds(1, 1), pl.ds(rows + 1, 1)
        return pltpu.make_async_remote_copy(
            src_ref=ref.at[2, source],
            dst_ref=ref.at[2 - j, target],
            send_sem=edge_send.at[which, index],
            recv_sem=edge_recv.at[which, index],
            device_id={"wide": w + toward * j, "narrow": n + toward * i},
            device_id_type=MESH,
        )

    def send_edges(which):
        for index, (j, i) in enumerate(edges):
            @pl.when(inside(w + j, n + i))
            def _():
                edge_copy(which, index).start()

    def fill_columns(which):
        for index, (j, i) in enumerate(edges):
            @pl.when(inside(w - j, n - i))
            def _():
                edge_copy(which, index, -1).wait_recv()
        ref = (frames, halo_out)[which]
        place = lax.broadcasted_iota(jnp.int32, (rows + 2, cols, chans), 1)
        place = place.reshape((rows + 2) * cols, chans)
        for a in range(3):
            flat = ref[a].reshape((rows + 2) * cols, chans)
            wider = flat.astype(jnp.float32)
            for e in range(3):
                if e == 0:
                    moved = jnp.where(place == 0, 0.0, pltpu.roll(wider, 1, 0))
                    moved = moved.astype(jnp.bfloat16)
                elif e == 1:
                    moved = flat
                else:
                    moved = pltpu.roll(wider, (rows + 2) * cols - 1, 0)
                    moved = jnp.where(place == cols - 1, 0.0, moved).astype(jnp.bfloat16)
                for b in range(3):
                    tap = 9 * a + 3 * b + e
                    columns[:, tap * chans : (tap + 1) * chans] = moved[
                        b * cols : (b + rows) * cols
                    ]

    def convolve(part):
        outs = wide * shapes[part][0]
        size = 3 * chans
        total[...] = jnp.zeros_like(total)

        def step(index, carry):
            at = pl.ds(pl.multiple_of(index * size, LANE), size)
            total[...] += lax.dot_general(
                columns[:, at],
                full[part][:, :, at].reshape(outs, size),
                (((1,), (1,)), ((), ())),
                preferred_element_type=jnp.float32,
            )
            return carry

        lax.fori_loop(0, 9, step, 0)

    strip_tokens = rows * cols // 4

    def strip_copy(kind):
        strip = {"core": n, "y": n, "relay": n + 2 - 4 * y}[kind]
        index = ("core", "y", "relay").index(kind)
        return pltpu.make_async_remote_copy(
            src_ref=patches.at[strip],
            dst_ref=patches.at[strip],
            send_sem=strip_send.at[index],
            recv_sem=strip_recv.at[index],
            device_id=peer_y if kind == "y" else peer_core,
            device_id_type=MESH,
        )

    def strip_landed(kind):
        strip = {"core": n + 1 - 2 * core, "y": n + 2 - 4 * y, "relay": 3 - n}[kind]
        index = ("core", "y", "relay").index(kind)
        return pltpu.make_async_remote_copy(
            src_ref=patches.at[strip],
            dst_ref=patches.at[strip],
            send_sem=strip_send.at[index],
            recv_sem=strip_recv.at[index],
            device_id=peer_y if kind == "y" else peer_core,
            device_id_type=MESH,
        )

    def first_conv():
        complete(0)
        convolve(0)
        outcome = total[...]
        outcome = outcome / (1.0 + jnp.exp(-outcome))
        halo_out[2, 1 : rows + 1] = outcome.astype(jnp.bfloat16).reshape(rows, cols, chans)
        send_edges(1)

    def second_conv():
        fill_columns(1)
        complete(1)
        convolve(1)
        result = total[...] + latent[0].reshape(rows * cols, chans).astype(jnp.float32)
        for part in range(chans // LANE):
            lanes[part] = result[:, part * LANE : (part + 1) * LANE]
        for b in range(2):
            for e in range(2):
                for part in range(chans // LANE):
                    pieces = [
                        lanes[part, pl.ds((2 * p + b) * cols + e, cols // 2, stride=2), :]
                        for p in range(rows // 2)
                    ]
                    at = (2 * b + e) * chans + part * LANE
                    patches[n, :, at : at + LANE] = jnp.concatenate(pieces, axis=0).astype(
                        jnp.bfloat16
                    )
        strip_copy("core").start()
        strip_copy("y").start()

    def window(part, shard, kind):
        half, third = strips(shapes[part][1])
        start, size = {
            "own": (core * half + y * third, half - third),
            "to_y": (core * half + y * (half - third), third),
            "from_y": (core * half + (1 - y) * (half - third), third),
            "core_own": ((1 - core) * half + y * third, half - third),
            "core_y": ((1 - core) * half + (1 - y) * (half - third), third),
        }[kind]
        cols = pl.ds(pl.multiple_of(start * LANE, LANE), size * LANE)
        return (shard, slice(None), cols)

    def transfer(part, shard, kind, lane, peer, own=False):
        at = window(part, shard, kind)
        target = full[part].at[at]
        source = mine[part].at[at[1:]] if own else target
        arrive = {"own": 0, "to_y": 1, "from_y": 3}[kind]
        if lane == "core" and kind == "own":
            arrive = 2
        send = ("up", "down", "x", "y", "core", "core_y").index(lane if kind != "from_y" else "core_y")
        return pltpu.make_async_remote_copy(
            src_ref=source,
            dst_ref=target,
            send_sem=send_sem.at[part, shard, send],
            recv_sem=recv_sem.at[part, shard, arrive],
            device_id=peer,
            device_id_type=MESH,
        )

    def landed(part, shard, kind):
        at = window(part, shard, kind)
        target = full[part].at[at]
        arrive = {"own": 0, "from_y": 1, "core_own": 2, "core_y": 3}[kind]
        return pltpu.make_async_remote_copy(
            src_ref=target,
            dst_ref=target,
            send_sem=send_sem.at[part, shard, 0],
            recv_sem=recv_sem.at[part, shard, arrive],
            device_id=peer_core,
            device_id_type=MESH,
        )

    def pass_on(part, shard):
        transfer(part, shard, "to_y", "y", peer_y).start()
        transfer(part, shard, "own", "core", peer_core).start()

    def from_partner(part, row):
        shard = 2 * row + 1 - x
        landed(part, shard, "own").wait_recv()
        pass_on(part, shard)

    def from_y(part, shard):
        landed(part, shard, "from_y").wait_recv()
        transfer(part, shard, "from_y", "core", peer_core).start()

    def stage(part, d):
        if d == 0:
            @pl.when(has_above)
            def _():
                transfer(part, w, "own", "up", above, own=True).start()

            @pl.when(has_below)
            def _():
                transfer(part, w, "own", "down", below, own=True).start()

            transfer(part, w, "own", "x", peer_x, own=True).start()
            pltpu.make_async_copy(mine[part], full[part].at[w], own_sem.at[part]).start()
            return

        @pl.when(z >= d)
        def _():
            shard = w - 2 * d
            landed(part, shard, "own").wait_recv()

            @pl.when(has_above)
            def _():
                transfer(part, shard, "own", "up", above).start()

            transfer(part, shard, "own", "x", peer_x).start()
            pass_on(part, shard)

        @pl.when(z + d < depth)
        def _():
            shard = w + 2 * d
            landed(part, shard, "own").wait_recv()

            @pl.when(has_below)
            def _():
                transfer(part, shard, "own", "down", below).start()

            transfer(part, shard, "own", "x", peer_x).start()
            pass_on(part, shard)

        late(part, d - 1)

    def late(part, d):
        for sign in (-1, 1) if d else (1,):
            row = z + sign * d

            @pl.when((row >= 0) & (row < depth))
            def _():
                from_partner(part, row)
        if d >= 1:
            later(part, d - 1)

    def later(part, d):
        for sign in (-1, 1) if d else (1,):
            row = z + sign * d

            @pl.when((row >= 0) & (row < depth))
            def _():
                if d:
                    from_y(part, 2 * row + x)
                from_y(part, 2 * row + 1 - x)

    def complete(part):
        pltpu.make_async_copy(mine[part], full[part].at[w], own_sem.at[part]).wait()
        for shard in range(wide):
            @pl.when(shard != w)
            def _():
                landed(part, shard, "core_own").wait_recv()
                landed(part, shard, "core_y").wait_recv()

    for tick in range(2 * count + depth):
        for part in range(count):
            d = tick - 2 * part
            if 0 <= d < depth:
                stage(part, d)
            elif d == depth:
                late(part, d - 1)
            elif d == depth + 1:
                later(part, d - 2)
        if tick == 0:
            send_edges(0)
        if tick == 2:
            fill_columns(0)
        if tick == depth + 1:
            first_conv()
        if tick == depth + 3:
            second_conv()
    strip_landed("y").wait_recv()
    strip_copy("relay").start()
    complete(2)
    strip_landed("core").wait_recv()
    strip_landed("relay").wait_recv()
    for kind in ("core", "y", "relay"):
        strip_copy(kind).wait_send()
    for which in range(2):
        for index, (j, i) in enumerate(edges):
            @pl.when(inside(w + j, n + i))
            def _():
                edge_copy(which, index).wait_send()
    for part in range(count):
        for row in range(depth):
            for side in range(2):
                shard = 2 * row + side

                @pl.when(shard != w)
                def _():
                    transfer(part, shard, "to_y", "y", peer_y).wait_send()
                    transfer(part, shard, "own", "core", peer_core).wait_send()
                    transfer(part, shard, "from_y", "core", peer_core).wait_send()

                @pl.when(side == x)
                def _():
                    transfer(part, shard, "own", "x", peer_x).wait_send()

                    @pl.when(has_above & (row <= z))
                    def _():
                        transfer(part, shard, "own", "up", above).wait_send()

                    @pl.when(has_below & (row >= z))
                    def _():
                        transfer(part, shard, "own", "down", below).wait_send()


def conv_block(latent, parts):
    wide, narrow = lax.axis_size("wide"), lax.axis_size("narrow")
    shapes = [part.shape for part in parts]
    count = len(parts)
    rows, cols, chans = latent.shape[1:]
    whole = [(wide,) + shape for shape in shapes]
    return pl.pallas_call(
        functools.partial(block_kernel, wide, narrow, shapes),
        out_shape=[
            jax.ShapeDtypeStruct((narrow, rows * cols // 4, 4 * chans), jnp.bfloat16),
            jax.ShapeDtypeStruct(whole[2], jnp.bfloat16),
        ],
        in_specs=[pl.BlockSpec(memory_space=pltpu.VMEM)]
        + [pl.BlockSpec(memory_space=pl.ANY)] * count,
        out_specs=[
            pl.BlockSpec(memory_space=pltpu.VMEM),
            pl.BlockSpec(memory_space=pl.ANY),
        ],
        scratch_shapes=[
            pltpu.VMEM(whole[0], jnp.bfloat16),
            pltpu.VMEM(whole[1], jnp.bfloat16),
            pltpu.VMEM((3, rows + 2, cols, chans), jnp.bfloat16),
            pltpu.VMEM((3, rows + 2, cols, chans), jnp.bfloat16),
            pltpu.VMEM((rows * cols, 27 * chans), jnp.bfloat16),
            pltpu.VMEM((rows * cols, chans), jnp.float32),
            pltpu.VMEM((chans // LANE, rows * cols, LANE), jnp.float32),
            pltpu.SemaphoreType.DMA((count,)),
            pltpu.SemaphoreType.DMA((count, wide, 6)),
            pltpu.SemaphoreType.DMA((count, wide, 4)),
            pltpu.SemaphoreType.DMA((2, 8)),
            pltpu.SemaphoreType.DMA((2, 8)),
            pltpu.SemaphoreType.DMA((3,)),
            pltpu.SemaphoreType.DMA((3,)),
        ],
        compiler_params=pltpu.CompilerParams(
            collective_id=0, has_side_effects=True, vmem_limit_bytes=40 * 1024 * 1024
        ),
    )(latent, *parts)


def shifted(x, axis, by):
    size = lax.axis_size(axis)
    pairs = [(i, i + by) for i in range(size) if 0 <= i + by < size]
    return lax.ppermute(x, axis, pairs)


def extended(block, sides, width):
    for axis, dim in sides:
        count = lax.axis_size(axis)
        forward = [(i, i + 1) for i in range(count - 1)]
        backward = [(target, source) for source, target in forward]
        low = lax.ppermute(
            lax.slice_in_dim(block, block.shape[dim] - width, None, axis=dim), axis, forward
        )
        high = lax.ppermute(lax.slice_in_dim(block, 0, width, axis=dim), axis, backward)
        block = jnp.concatenate([low, block, high], axis=dim)
    return block


def causal_conv(current, weight):
    before = shifted(current, "wide", 1)
    earlier = shifted(current, "wide", 2)
    stacked = jnp.concatenate([earlier, before, current], axis=0)
    rimmed = extended(stacked, (("narrow", 1),), 1)
    padded = jnp.pad(rimmed, ((0, 0), (0, 0), (1, 1), (0, 0)))
    row_count = current.shape[1]
    col_count = current.shape[2]
    chan_count = current.shape[3]
    block_cols = lax.all_gather(weight, "wide", axis=1, tiled=True)
    summed = jnp.zeros((row_count * col_count, block_cols.shape[1]), jnp.float32)
    for kernel_tap in range(27):
        time_step = kernel_tap // 9
        row_step = kernel_tap // 3 % 3
        col_step = kernel_tap % 3
        window = padded[time_step, row_step : row_step + row_count, col_step : col_step + col_count]
        window = window.reshape(row_count * col_count, chan_count)
        summed = summed + jnp.dot(
            window,
            block_cols[kernel_tap * chan_count : (kernel_tap + 1) * chan_count],
            preferred_element_type=jnp.float32,
        )
    return summed


def embed_tokens(patch_feats, embed_weight):
    return jnp.dot(
        patch_feats,
        lax.all_gather(embed_weight, "wide", axis=1, tiled=True),
        preferred_element_type=jnp.float32,
    ).astype(jnp.bfloat16)


def embedded_plain(latent, conv_first, conv_second, embed_weight):
    row_count = latent.shape[1]
    col_count = latent.shape[2]
    chan_count = latent.shape[3]
    first = causal_conv(latent, conv_first)
    activated = jax.nn.silu(first).astype(jnp.bfloat16).reshape(latent.shape)
    second = causal_conv(activated, conv_second) + latent.reshape(-1, chan_count).astype(
        jnp.float32
    )
    block_out = second.astype(jnp.bfloat16)
    patches = block_out.reshape(row_count // 2, 2, col_count // 2, 2, chan_count)
    patches = patches.transpose(0, 2, 1, 3, 4).reshape(-1, 4 * chan_count)
    return lax.all_gather(embed_tokens(patches, embed_weight), "narrow", axis=0, tiled=True)


def embedded_fused(latent, conv_first, conv_second, embed_weight):
    patches, weights = conv_block(latent, [conv_first.T, conv_second.T, embed_weight.T])
    return lax.dot_general(
        patches.reshape(-1, patches.shape[2]),
        weights.reshape(-1, weights.shape[2]),
        (((1,), (1,)), ((), ())),
        preferred_element_type=jnp.float32,
    ).astype(jnp.bfloat16)


def per_device(latent, conv_first, conv_second, embed_weight, qkv_weight):
    wide, narrow = lax.axis_size("wide"), lax.axis_size("narrow")
    fits = narrow == 4 and wide % 2 == 0 and conv_first.shape[1] % 16 == 0
    embed = embedded_fused if fits else embedded_plain
    embedded = embed(latent, conv_first, conv_second, embed_weight)
    heads_here = qkv_weight.shape[2] // HEAD_DIM
    token_count = embedded.shape[0]
    query_raw = jnp.dot(embedded, qkv_weight[0], preferred_element_type=jnp.float32)
    key_raw = jnp.dot(embedded, qkv_weight[1], preferred_element_type=jnp.float32)
    val_rows = jnp.dot(embedded, qkv_weight[2], preferred_element_type=jnp.float32).astype(
        jnp.bfloat16
    )
    query_feat = (
        (jax.nn.elu(query_raw) + 1.0)
        .astype(jnp.bfloat16)
        .reshape(token_count, heads_here, HEAD_DIM)
    )
    key_feat = (
        (jax.nn.elu(key_raw) + 1.0).astype(jnp.bfloat16).reshape(token_count, heads_here, HEAD_DIM)
    )
    val_heads = val_rows.reshape(token_count, heads_here, HEAD_DIM)
    scores = jnp.einsum("thd,shd->hts", query_feat, key_feat, preferred_element_type=jnp.float32)
    row_ids = lax.broadcasted_iota(jnp.int32, (token_count, token_count), 0)
    col_ids = lax.broadcasted_iota(jnp.int32, (token_count, token_count), 1)
    scores = jnp.where((col_ids <= row_ids)[None], scores, 0.0)
    local_den = jnp.sum(scores, axis=-1)
    local_num = jnp.einsum(
        "hts,she->the", scores.astype(jnp.bfloat16), val_heads, preferred_element_type=jnp.float32
    )
    state_local = jnp.einsum(
        "thd,the->hde", key_feat, val_heads, preferred_element_type=jnp.float32
    )
    key_local = jnp.sum(key_feat, axis=0, dtype=jnp.float32)
    flat_state = jnp.concatenate([state_local.reshape(-1), key_local.reshape(-1)])
    length_all = flat_state.shape[0]
    peer_count = lax.axis_size("wide")
    per_peer = -(-length_all // peer_count)
    piece_grid = jnp.pad(flat_state, (0, per_peer * peer_count - length_all)).reshape(
        peer_count, per_peer
    )
    lower_ones = (
        lax.broadcasted_iota(jnp.int32, (peer_count, peer_count), 1)
        < lax.broadcasted_iota(jnp.int32, (peer_count, peer_count), 0)
    ).astype(jnp.float32)
    partial_sums = jnp.dot(
        lower_ones,
        lax.all_to_all(
            piece_grid.astype(jnp.bfloat16), "wide", split_axis=0, concat_axis=0, tiled=True
        ).astype(piece_grid.dtype),
        precision=lax.Precision.HIGHEST,
    )
    spread = lax.all_to_all(
        partial_sums.astype(jnp.bfloat16), "wide", split_axis=0, concat_axis=0, tiled=True
    ).astype(partial_sums.dtype)
    flat_prefix = spread.reshape(-1)[:length_all]
    state_size = state_local.size
    state_prev = flat_prefix[:state_size].reshape(state_local.shape)
    key_prev = flat_prefix[state_size:].reshape(key_local.shape)
    query_wide = query_feat.astype(jnp.float32)
    carried_num = jnp.einsum(
        "thd,hde->the", query_wide, state_prev, precision=lax.Precision.HIGHEST
    )
    carried_den = jnp.einsum("thd,hd->th", query_wide, key_prev, precision=lax.Precision.HIGHEST)
    result = (local_num + carried_num) / (local_den.T + carried_den)[..., None]
    return result.astype(jnp.bfloat16).reshape(token_count, heads_here * HEAD_DIM)


def solution(mesh):
    return jax.shard_map(
        per_device,
        mesh=mesh,
        in_specs=(
            P("wide", "narrow", None, None),
            P(None, "wide"),
            P(None, "wide"),
            P(None, "wide"),
            P(None, None, "narrow"),
        ),
        out_specs=P("wide", "narrow"),
        check_vma=False,
    )
```

```python
import functools

import jax
import jax.numpy as jnp
from jax import lax
from jax.experimental import pallas as pl
from jax.experimental.pallas import tpu as pltpu
from jax.sharding import PartitionSpec as P

HEAD_DIM = 112
LANE = 128
MESH = pl.DeviceIdType.MESH


def strips(lanes):
    half = lanes // LANE // 2
    return half, max(1, half // 3)


def block_kernel(
    wide, narrow, shapes, latent, first_w, second_w, embed_w, patches, embed_full,
    first_full, second_full, frames, halo_out, columns, total, lanes, own_sem, send_sem, recv_sem,
    edge_send, edge_recv, strip_send, strip_recv,
):
    count = len(shapes)
    mine = (first_w, second_w, embed_w)
    full = (first_full, second_full, embed_full)
    rows, cols, chans = latent.shape[1:]
    frames[...] = jnp.zeros_like(frames)
    halo_out[...] = jnp.zeros_like(halo_out)
    frames[2, 1 : rows + 1] = latent[0]
    w = lax.axis_index("wide")
    n = lax.axis_index("narrow")
    z, x = w // 2, lax.rem(w, 2)
    y, core = lax.rem(n // 2, 2), lax.rem(n, 2)
    depth = wide // 2
    peer_x = {"wide": w + 1 - 2 * x}
    peer_y = {"narrow": n + 2 - 4 * y}
    peer_core = {"narrow": n + 1 - 2 * core}
    above, below = {"wide": w + 2}, {"wide": w - 2}
    has_above, has_below = z < depth - 1, z > 0

    barrier = pltpu.get_barrier_semaphore()
    for peer in (peer_x, peer_y, peer_core):
        pl.semaphore_signal(barrier, inc=1, device_id=peer, device_id_type=MESH)

    @pl.when(has_above)
    def _():
        pl.semaphore_signal(barrier, inc=1, device_id=above, device_id_type=MESH)

    @pl.when(has_below)
    def _():
        pl.semaphore_signal(barrier, inc=1, device_id=below, device_id_type=MESH)

    def inside(frame, strip):
        return (frame >= 0) & (frame < wide) & (strip >= 0) & (strip < narrow)

    edges = [(j, i) for j in (2, 1, 0) for i in (0, -1, 1) if (j, i) != (0, 0)]
    expected = 3 + has_above.astype(jnp.int32) + has_below.astype(jnp.int32)
    for j, i in edges:
        @pl.when(inside(w - j, n - i))
        def _():
            pl.semaphore_signal(
                barrier, inc=1, device_id={"wide": w - j, "narrow": n - i}, device_id_type=MESH
            )

        expected = expected + inside(w + j, n + i).astype(jnp.int32)
    pl.semaphore_wait(barrier, expected)

    def edge_copy(which, index, toward=1):
        j, i = edges[index]
        ref = (frames, halo_out)[which]
        if i == 0:
            source, target = pl.ds(1, rows), pl.ds(1, rows)
        elif i == 1:
            source, target = pl.ds(rows, 1), pl.ds(0, 1)
        else:
            source, target = pl.ds(1, 1), pl.ds(rows + 1, 1)
        return pltpu.make_async_remote_copy(
            src_ref=ref.at[2, source],
            dst_ref=ref.at[2 - j, target],
            send_sem=edge_send.at[which, index],
            recv_sem=edge_recv.at[which, index],
            device_id={"wide": w + toward * j, "narrow": n + toward * i},
            device_id_type=MESH,
        )

    def send_edges(which):
        for index, (j, i) in enumerate(edges):
            @pl.when(inside(w + j, n + i))
            def _():
                edge_copy(which, index).start()

    def fill_columns(which):
        for index, (j, i) in enumerate(edges):
            @pl.when(inside(w - j, n - i))
            def _():
                edge_copy(which, index, -1).wait_recv()
        ref = (frames, halo_out)[which]
        place = lax.broadcasted_iota(jnp.int32, (rows + 2, cols, chans), 1)
        place = place.reshape((rows + 2) * cols, chans)
        for a in range(3):
            flat = ref[a].reshape((rows + 2) * cols, chans)
            wider = flat.astype(jnp.float32)
            for e in range(3):
                if e == 0:
                    moved = jnp.where(place == 0, 0.0, pltpu.roll(wider, 1, 0))
                    moved = moved.astype(jnp.bfloat16)
                elif e == 1:
                    moved = flat
                else:
                    moved = pltpu.roll(wider, (rows + 2) * cols - 1, 0)
                    moved = jnp.where(place == cols - 1, 0.0, moved).astype(jnp.bfloat16)
                for b in range(3):
                    tap = 9 * a + 3 * b + e
                    columns[:, tap * chans : (tap + 1) * chans] = moved[
                        b * cols : (b + rows) * cols
                    ]

    def convolve(part):
        outs = wide * shapes[part][0]
        size = 3 * chans
        total[...] = jnp.zeros_like(total)

        def step(index, carry):
            at = pl.ds(pl.multiple_of(index * size, LANE), size)
            total[...] += lax.dot_general(
                columns[:, at],
                full[part][:, :, at].reshape(outs, size),
                (((1,), (1,)), ((), ())),
                preferred_element_type=jnp.float32,
            )
            return carry

        lax.fori_loop(0, 9, step, 0)

    strip_tokens = rows * cols // 4

    def strip_copy(kind):
        strip = {"core": n, "y": n, "relay": n + 2 - 4 * y}[kind]
        index = ("core", "y", "relay").index(kind)
        return pltpu.make_async_remote_copy(
            src_ref=patches.at[strip],
            dst_ref=patches.at[strip],
            send_sem=strip_send.at[index],
            recv_sem=strip_recv.at[index],
            device_id=peer_y if kind == "y" else peer_core,
            device_id_type=MESH,
        )

    def strip_landed(kind):
        strip = {"core": n + 1 - 2 * core, "y": n + 2 - 4 * y, "relay": 3 - n}[kind]
        index = ("core", "y", "relay").index(kind)
        return pltpu.make_async_remote_copy(
            src_ref=patches.at[strip],
            dst_ref=patches.at[strip],
            send_sem=strip_send.at[index],
            recv_sem=strip_recv.at[index],
            device_id=peer_y if kind == "y" else peer_core,
            device_id_type=MESH,
        )

    def first_conv():
        complete(0)
        convolve(0)
        outcome = total[...]
        outcome = outcome / (1.0 + jnp.exp(-outcome))
        halo_out[2, 1 : rows + 1] = outcome.astype(jnp.bfloat16).reshape(rows, cols, chans)
        send_edges(1)

    def second_conv():
        fill_columns(1)
        complete(1)
        convolve(1)
        result = total[...] + latent[0].reshape(rows * cols, chans).astype(jnp.float32)
        for part in range(chans // LANE):
            lanes[part] = result[:, part * LANE : (part + 1) * LANE]
        for b in range(2):
            for e in range(2):
                for part in range(chans // LANE):
                    pieces = [
                        lanes[part, pl.ds((2 * p + b) * cols + e, cols // 2, stride=2), :]
                        for p in range(rows // 2)
                    ]
                    at = (2 * b + e) * chans + part * LANE
                    patches[n, :, at : at + LANE] = jnp.concatenate(pieces, axis=0).astype(
                        jnp.bfloat16
                    )
        strip_copy("core").start()
        strip_copy("y").start()

    def window(part, shard, kind):
        half, third = strips(shapes[part][1])
        start, size = {
            "own": (core * half + y * third, half - third),
            "to_y": (core * half + y * (half - third), third),
            "from_y": (core * half + (1 - y) * (half - third), third),
            "core_own": ((1 - core) * half + y * third, half - third),
            "core_y": ((1 - core) * half + (1 - y) * (half - third), third),
        }[kind]
        cols = pl.ds(pl.multiple_of(start * LANE, LANE), size * LANE)
        return (shard, slice(None), cols)

    def transfer(part, shard, kind, lane, peer, own=False):
        at = window(part, shard, kind)
        target = full[part].at[at]
        source = mine[part].at[at[1:]] if own else target
        arrive = {"own": 0, "to_y": 1, "from_y": 3}[kind]
        if lane == "core" and kind == "own":
            arrive = 2
        send = ("up", "down", "x", "y", "core", "core_y").index(lane if kind != "from_y" else "core_y")
        return pltpu.make_async_remote_copy(
            src_ref=source,
            dst_ref=target,
            send_sem=send_sem.at[part, shard, send],
            recv_sem=recv_sem.at[part, shard, arrive],
            device_id=peer,
            device_id_type=MESH,
        )

    def landed(part, shard, kind):
        at = window(part, shard, kind)
        target = full[part].at[at]
        arrive = {"own": 0, "from_y": 1, "core_own": 2, "core_y": 3}[kind]
        return pltpu.make_async_remote_copy(
            src_ref=target,
            dst_ref=target,
            send_sem=send_sem.at[part, shard, 0],
            recv_sem=recv_sem.at[part, shard, arrive],
            device_id=peer_core,
            device_id_type=MESH,
        )

    def pass_on(part, shard):
        transfer(part, shard, "to_y", "y", peer_y).start()
        transfer(part, shard, "own", "core", peer_core).start()

    def from_partner(part, row):
        shard = 2 * row + 1 - x
        landed(part, shard, "own").wait_recv()
        pass_on(part, shard)

    def from_y(part, shard):
        landed(part, shard, "from_y").wait_recv()
        transfer(part, shard, "from_y", "core", peer_core).start()

    def stage(part, d):
        if d == 0:
            @pl.when(has_above)
            def _():
                transfer(part, w, "own", "up", above, own=True).start()

            @pl.when(has_below)
            def _():
                transfer(part, w, "own", "down", below, own=True).start()

            transfer(part, w, "own", "x", peer_x, own=True).start()
            pltpu.make_async_copy(mine[part], full[part].at[w], own_sem.at[part]).start()
            return

        @pl.when(z >= d)
        def _():
            shard = w - 2 * d
            landed(part, shard, "own").wait_recv()

            @pl.when(has_above)
            def _():
                transfer(part, shard, "own", "up", above).start()

            transfer(part, shard, "own", "x", peer_x).start()
            pass_on(part, shard)

        @pl.when(z + d < depth)
        def _():
            shard = w + 2 * d
            landed(part, shard, "own").wait_recv()

            @pl.when(has_below)
            def _():
                transfer(part, shard, "own", "down", below).start()

            transfer(part, shard, "own", "x", peer_x).start()
            pass_on(part, shard)

        late(part, d - 1)

    def late(part, d):
        for sign in (-1, 1) if d else (1,):
            row = z + sign * d

            @pl.when((row >= 0) & (row < depth))
            def _():
                from_partner(part, row)
        if d >= 1:
            later(part, d - 1)

    def later(part, d):
        for sign in (-1, 1) if d else (1,):
            row = z + sign * d

            @pl.when((row >= 0) & (row < depth))
            def _():
                if d:
                    from_y(part, 2 * row + x)
                from_y(part, 2 * row + 1 - x)

    def complete(part):
        pltpu.make_async_copy(mine[part], full[part].at[w], own_sem.at[part]).wait()
        for shard in range(wide):
            @pl.when(shard != w)
            def _():
                landed(part, shard, "core_own").wait_recv()
                landed(part, shard, "core_y").wait_recv()

    begins = (0, 1, 3)
    for tick in range(begins[-1] + depth + 2):
        for part in range(count):
            d = tick - begins[part]
            if 0 <= d < depth:
                stage(part, d)
            elif d == depth:
                late(part, d - 1)
            elif d == depth + 1:
                later(part, d - 2)
        if tick == 0:
            send_edges(0)
        if tick == 2:
            fill_columns(0)
        if tick == depth + 1:
            first_conv()
        if tick == depth + 3:
            second_conv()
    strip_landed("y").wait_recv()
    strip_copy("relay").start()
    complete(2)
    strip_landed("core").wait_recv()
    strip_landed("relay").wait_recv()
    for kind in ("core", "y", "relay"):
        strip_copy(kind).wait_send()
    for which in range(2):
        for index, (j, i) in enumerate(edges):
            @pl.when(inside(w + j, n + i))
            def _():
                edge_copy(which, index).wait_send()
    for part in range(count):
        for row in range(depth):
            for side in range(2):
                shard = 2 * row + side

                @pl.when(shard != w)
                def _():
                    transfer(part, shard, "to_y", "y", peer_y).wait_send()
                    transfer(part, shard, "own", "core", peer_core).wait_send()
                    transfer(part, shard, "from_y", "core", peer_core).wait_send()

                @pl.when(side == x)
                def _():
                    transfer(part, shard, "own", "x", peer_x).wait_send()

                    @pl.when(has_above & (row <= z))
                    def _():
                        transfer(part, shard, "own", "up", above).wait_send()

                    @pl.when(has_below & (row >= z))
                    def _():
                        transfer(part, shard, "own", "down", below).wait_send()


def conv_block(latent, parts):
    wide, narrow = lax.axis_size("wide"), lax.axis_size("narrow")
    shapes = [part.shape for part in parts]
    count = len(parts)
    rows, cols, chans = latent.shape[1:]
    whole = [(wide,) + shape for shape in shapes]
    return pl.pallas_call(
        functools.partial(block_kernel, wide, narrow, shapes),
        out_shape=[
            jax.ShapeDtypeStruct((narrow, rows * cols // 4, 4 * chans), jnp.bfloat16),
            jax.ShapeDtypeStruct(whole[2], jnp.bfloat16),
        ],
        in_specs=[pl.BlockSpec(memory_space=pltpu.VMEM)]
        + [pl.BlockSpec(memory_space=pltpu.HBM)] * count,
        out_specs=[
            pl.BlockSpec(memory_space=pltpu.VMEM),
            pl.BlockSpec(memory_space=pl.ANY),
        ],
        scratch_shapes=[
            pltpu.VMEM(whole[0], jnp.bfloat16),
            pltpu.VMEM(whole[1], jnp.bfloat16),
            pltpu.VMEM((3, rows + 2, cols, chans), jnp.bfloat16),
            pltpu.VMEM((3, rows + 2, cols, chans), jnp.bfloat16),
            pltpu.VMEM((rows * cols, 27 * chans), jnp.bfloat16),
            pltpu.VMEM((rows * cols, chans), jnp.float32),
            pltpu.VMEM((chans // LANE, rows * cols, LANE), jnp.float32),
            pltpu.SemaphoreType.DMA((count,)),
            pltpu.SemaphoreType.DMA((count, wide, 6)),
            pltpu.SemaphoreType.DMA((count, wide, 4)),
            pltpu.SemaphoreType.DMA((2, 8)),
            pltpu.SemaphoreType.DMA((2, 8)),
            pltpu.SemaphoreType.DMA((3,)),
            pltpu.SemaphoreType.DMA((3,)),
        ],
        compiler_params=pltpu.CompilerParams(
            collective_id=0, has_side_effects=True, vmem_limit_bytes=40 * 1024 * 1024
        ),
    )(latent, *parts)


def mix_kernel(
    wide, size, query, key, value, mixed,
    states, came, prefix, back, local, out_sem, in_sem,
):
    w = lax.axis_index("wide")
    heads, tokens, lanes = query.shape
    piece = states.shape[1]
    barrier = pltpu.get_barrier_semaphore()

    def peer(step):
        return lax.rem(w + step, wide)

    for step in range(1, wide):
        pl.semaphore_signal(
            barrier, inc=1, device_id={"wide": peer(step)}, device_id_type=MESH
        )

    for head in range(heads):
        outer = lax.dot_general(
            key[head], value[head], (((0,), (0,)), ((), ())), preferred_element_type=jnp.float32
        ).astype(jnp.bfloat16)
        for row in range(0, lanes, 16):
            index, at = divmod(head * lanes + row, piece)
            states[index, at : at + 16] = outer[row : row + 16]

    def push(phase, step):
        to = peer(step)
        source, target = ((states, came), (prefix, back))[phase]
        return pltpu.make_async_remote_copy(
            src_ref=source.at[to],
            dst_ref=target.at[w],
            send_sem=out_sem.at[phase, step],
            recv_sem=in_sem.at[phase, step],
            device_id={"wide": to},
            device_id_type=MESH,
        )

    def arrived(phase, step):
        sender = lax.rem(w + wide - step, wide)
        target = (came, back)[phase]
        return pltpu.make_async_remote_copy(
            src_ref=target.at[sender],
            dst_ref=target.at[sender],
            send_sem=out_sem.at[phase, step],
            recv_sem=in_sem.at[phase, step],
            device_id={"wide": sender},
            device_id_type=MESH,
        )

    row_ids = lax.broadcasted_iota(jnp.int32, (tokens, tokens), 0)
    col_ids = lax.broadcasted_iota(jnp.int32, (tokens, tokens), 1)
    spot = lax.broadcasted_iota(jnp.int32, (tokens, lanes), 1)

    def inside_frame(head):
        scores = lax.dot_general(
            query[head], key[head], (((1,), (1,)), ((), ())), preferred_element_type=jnp.float32
        )
        scores = jnp.where(col_ids <= row_ids, scores, 0.0)
        below = jnp.sum(scores, axis=1, keepdims=True)
        above = jnp.dot(
            scores.astype(jnp.bfloat16), value[head], preferred_element_type=jnp.float32
        )
        local[head] = jnp.where(spot == size, below, above)

    pl.semaphore_wait(barrier, wide - 1)
    for step in range(1, wide):
        push(0, step).start()
    came[w] = states[w]
    for head in range(heads // 2):
        inside_frame(head)
    for step in range(1, wide):
        arrived(0, step).wait_recv()
    running = jnp.zeros(states.shape[1:], jnp.float32)
    for frame in range(wide):
        prefix[frame] = running.astype(jnp.bfloat16)
        running = running + came[frame].astype(jnp.float32)
    for step in range(1, wide):
        push(1, step).start()
    back[w] = prefix[w]
    for head in range(heads // 2, heads):
        inside_frame(head)
    for step in range(1, wide):
        arrived(1, step).wait_recv()
    for head in range(heads):
        parts = []
        for row in range(0, lanes, 16):
            index, at = divmod(head * lanes + row, piece)
            parts.append(back[index, at : at + 16])
        carried = jnp.dot(
            query[head], jnp.concatenate(parts, axis=0), preferred_element_type=jnp.float32
        )
        whole = local[head] + carried
        mixed[head] = (whole / whole[:, size : size + 1]).astype(jnp.bfloat16)
    for phase in range(2):
        for step in range(1, wide):
            push(phase, step).wait_send()


def mix_frames(query, key, value, size):
    wide = lax.axis_size("wide")
    heads, tokens, lanes = query.shape
    pieces = (wide, heads * lanes // wide, lanes)
    return pl.pallas_call(
        functools.partial(mix_kernel, wide, size),
        out_shape=jax.ShapeDtypeStruct(query.shape, jnp.bfloat16),
        in_specs=[pl.BlockSpec(memory_space=pltpu.VMEM)] * 3,
        out_specs=pl.BlockSpec(memory_space=pltpu.VMEM),
        scratch_shapes=[
            pltpu.VMEM(pieces, jnp.bfloat16),
            pltpu.VMEM(pieces, jnp.bfloat16),
            pltpu.VMEM(pieces, jnp.bfloat16),
            pltpu.VMEM(pieces, jnp.bfloat16),
            pltpu.VMEM(query.shape, jnp.float32),
            pltpu.SemaphoreType.DMA((2, wide)),
            pltpu.SemaphoreType.DMA((2, wide)),
        ],
        compiler_params=pltpu.CompilerParams(
            collective_id=1, has_side_effects=True, vmem_limit_bytes=32 * 1024 * 1024
        ),
    )(query, key, value)


def shifted(x, axis, by):
    size = lax.axis_size(axis)
    pairs = [(i, i + by) for i in range(size) if 0 <= i + by < size]
    return lax.ppermute(x, axis, pairs)


def extended(block, sides, width):
    for axis, dim in sides:
        count = lax.axis_size(axis)
        forward = [(i, i + 1) for i in range(count - 1)]
        backward = [(target, source) for source, target in forward]
        low = lax.ppermute(
            lax.slice_in_dim(block, block.shape[dim] - width, None, axis=dim), axis, forward
        )
        high = lax.ppermute(lax.slice_in_dim(block, 0, width, axis=dim), axis, backward)
        block = jnp.concatenate([low, block, high], axis=dim)
    return block


def causal_conv(current, weight):
    before = shifted(current, "wide", 1)
    earlier = shifted(current, "wide", 2)
    stacked = jnp.concatenate([earlier, before, current], axis=0)
    rimmed = extended(stacked, (("narrow", 1),), 1)
    padded = jnp.pad(rimmed, ((0, 0), (0, 0), (1, 1), (0, 0)))
    row_count = current.shape[1]
    col_count = current.shape[2]
    chan_count = current.shape[3]
    block_cols = lax.all_gather(weight, "wide", axis=1, tiled=True)
    summed = jnp.zeros((row_count * col_count, block_cols.shape[1]), jnp.float32)
    for kernel_tap in range(27):
        time_step = kernel_tap // 9
        row_step = kernel_tap // 3 % 3
        col_step = kernel_tap % 3
        window = padded[time_step, row_step : row_step + row_count, col_step : col_step + col_count]
        window = window.reshape(row_count * col_count, chan_count)
        summed = summed + jnp.dot(
            window,
            block_cols[kernel_tap * chan_count : (kernel_tap + 1) * chan_count],
            preferred_element_type=jnp.float32,
        )
    return summed


def embed_tokens(patch_feats, embed_weight):
    return jnp.dot(
        patch_feats,
        lax.all_gather(embed_weight, "wide", axis=1, tiled=True),
        preferred_element_type=jnp.float32,
    ).astype(jnp.bfloat16)


def embedded_plain(latent, conv_first, conv_second, embed_weight):
    row_count = latent.shape[1]
    col_count = latent.shape[2]
    chan_count = latent.shape[3]
    first = causal_conv(latent, conv_first)
    activated = jax.nn.silu(first).astype(jnp.bfloat16).reshape(latent.shape)
    second = causal_conv(activated, conv_second) + latent.reshape(-1, chan_count).astype(
        jnp.float32
    )
    block_out = second.astype(jnp.bfloat16)
    patches = block_out.reshape(row_count // 2, 2, col_count // 2, 2, chan_count)
    patches = patches.transpose(0, 2, 1, 3, 4).reshape(-1, 4 * chan_count)
    return lax.all_gather(embed_tokens(patches, embed_weight), "narrow", axis=0, tiled=True)


def embedded_fused(latent, conv_first, conv_second, embed_weight):
    patches, weights = conv_block(latent, [conv_first.T, conv_second.T, embed_weight.T])
    return lax.dot_general(
        patches.reshape(-1, patches.shape[2]),
        weights.reshape(-1, weights.shape[2]),
        (((1,), (1,)), ((), ())),
        preferred_element_type=jnp.float32,
    ).astype(jnp.bfloat16)


def per_device(latent, conv_first, conv_second, embed_weight, qkv_weight):
    wide, narrow = lax.axis_size("wide"), lax.axis_size("narrow")
    fits = narrow == 4 and wide % 2 == 0 and conv_first.shape[1] % 16 == 0
    embed = embedded_fused if fits else embedded_plain
    embedded = embed(latent, conv_first, conv_second, embed_weight)
    heads_here = qkv_weight.shape[2] // HEAD_DIM
    token_count = embedded.shape[0]
    query_raw = jnp.dot(embedded, qkv_weight[0], preferred_element_type=jnp.float32)
    key_raw = jnp.dot(embedded, qkv_weight[1], preferred_element_type=jnp.float32)
    val_rows = jnp.dot(embedded, qkv_weight[2], preferred_element_type=jnp.float32).astype(
        jnp.bfloat16
    )
    query_feat = (
        (jax.nn.elu(query_raw) + 1.0)
        .astype(jnp.bfloat16)
        .reshape(token_count, heads_here, HEAD_DIM)
    )
    key_feat = (
        (jax.nn.elu(key_raw) + 1.0).astype(jnp.bfloat16).reshape(token_count, heads_here, HEAD_DIM)
    )
    val_heads = val_rows.reshape(token_count, heads_here, HEAD_DIM)
    if wide * 16 <= heads_here * LANE and heads_here * LANE % (wide * 16) == 0:

        def padded(rows):
            return jnp.pad(rows, ((0, 0), (0, 0), (0, LANE - HEAD_DIM))).transpose(1, 0, 2)

        place = lax.broadcasted_iota(jnp.int32, (heads_here, token_count, LANE), 2)
        value = jnp.where(place == HEAD_DIM, jnp.bfloat16(1), padded(val_heads))
        mixed = mix_frames(padded(query_feat), padded(key_feat), value, HEAD_DIM)
        return mixed.transpose(1, 0, 2)[:, :, :HEAD_DIM].reshape(token_count, -1)
    scores = jnp.einsum("thd,shd->hts", query_feat, key_feat, preferred_element_type=jnp.float32)
    row_ids = lax.broadcasted_iota(jnp.int32, (token_count, token_count), 0)
    col_ids = lax.broadcasted_iota(jnp.int32, (token_count, token_count), 1)
    scores = jnp.where((col_ids <= row_ids)[None], scores, 0.0)
    local_den = jnp.sum(scores, axis=-1)
    local_num = jnp.einsum(
        "hts,she->the", scores.astype(jnp.bfloat16), val_heads, preferred_element_type=jnp.float32
    )
    state_local = jnp.einsum(
        "thd,the->hde", key_feat, val_heads, preferred_element_type=jnp.float32
    )
    key_local = jnp.sum(key_feat, axis=0, dtype=jnp.float32)
    flat_state = jnp.concatenate([state_local.reshape(-1), key_local.reshape(-1)])
    length_all = flat_state.shape[0]
    peer_count = lax.axis_size("wide")
    per_peer = -(-length_all // peer_count)
    piece_grid = jnp.pad(flat_state, (0, per_peer * peer_count - length_all)).reshape(
        peer_count, per_peer
    )
    lower_ones = (
        lax.broadcasted_iota(jnp.int32, (peer_count, peer_count), 1)
        < lax.broadcasted_iota(jnp.int32, (peer_count, peer_count), 0)
    ).astype(jnp.float32)
    partial_sums = jnp.dot(
        lower_ones,
        lax.all_to_all(
            piece_grid.astype(jnp.bfloat16), "wide", split_axis=0, concat_axis=0, tiled=True
        ).astype(piece_grid.dtype),
        precision=lax.Precision.HIGHEST,
    )
    spread = lax.all_to_all(
        partial_sums.astype(jnp.bfloat16), "wide", split_axis=0, concat_axis=0, tiled=True
    ).astype(partial_sums.dtype)
    flat_prefix = spread.reshape(-1)[:length_all]
    state_size = state_local.size
    state_prev = flat_prefix[:state_size].reshape(state_local.shape)
    key_prev = flat_prefix[state_size:].reshape(key_local.shape)
    query_wide = query_feat.astype(jnp.float32)
    carried_num = jnp.einsum(
        "thd,hde->the", query_wide, state_prev, precision=lax.Precision.HIGHEST
    )
    carried_den = jnp.einsum("thd,hd->th", query_wide, key_prev, precision=lax.Precision.HIGHEST)
    result = (local_num + carried_num) / (local_den.T + carried_den)[..., None]
    return result.astype(jnp.bfloat16).reshape(token_count, heads_here * HEAD_DIM)


def solution(mesh):
    return jax.shard_map(
        per_device,
        mesh=mesh,
        in_specs=(
            P("wide", "narrow", None, None),
            P(None, "wide"),
            P(None, "wide"),
            P(None, "wide"),
            P(None, None, "narrow"),
        ),
        out_specs=P("wide", "narrow"),
        check_vma=False,
    )
```

```python
import functools

import jax
import jax.numpy as jnp
from jax import lax
from jax.experimental import pallas as pl
from jax.experimental.pallas import tpu as pltpu
from jax.sharding import PartitionSpec as P

HEAD_DIM = 112
LANE = 128
MESH = pl.DeviceIdType.MESH


def strips(lanes):
    half = lanes // LANE // 2
    return half, max(1, half * 41 // 100)


def block_kernel(
    wide, narrow, shapes, latent, first_w, second_w, embed_w, patches, embed_full,
    first_full, second_full, frames, halo_out, columns, total, lanes, own_sem, send_sem, recv_sem,
    edge_send, edge_recv, strip_send, strip_recv,
):
    count = len(shapes)
    mine = (first_w, second_w, embed_w)
    full = (first_full, second_full, embed_full)
    rows, cols, chans = latent.shape[1:]
    frames[...] = jnp.zeros_like(frames)
    halo_out[...] = jnp.zeros_like(halo_out)
    frames[2, 1 : rows + 1] = latent[0]
    w = lax.axis_index("wide")
    n = lax.axis_index("narrow")
    z, x = w // 2, lax.rem(w, 2)
    y, core = lax.rem(n // 2, 2), lax.rem(n, 2)
    depth = wide // 2
    peer_x = {"wide": w + 1 - 2 * x}
    peer_y = {"narrow": n + 2 - 4 * y}
    peer_core = {"narrow": n + 1 - 2 * core}
    above, below = {"wide": w + 2}, {"wide": w - 2}
    has_above, has_below = z < depth - 1, z > 0

    barrier = pltpu.get_barrier_semaphore()
    for peer in (peer_x, peer_y, peer_core):
        pl.semaphore_signal(barrier, inc=1, device_id=peer, device_id_type=MESH)

    @pl.when(has_above)
    def _():
        pl.semaphore_signal(barrier, inc=1, device_id=above, device_id_type=MESH)

    @pl.when(has_below)
    def _():
        pl.semaphore_signal(barrier, inc=1, device_id=below, device_id_type=MESH)

    def inside(frame, strip):
        return (frame >= 0) & (frame < wide) & (strip >= 0) & (strip < narrow)

    edges = [(j, i) for j in (2, 1, 0) for i in (0, -1, 1) if (j, i) != (0, 0)]
    expected = 3 + has_above.astype(jnp.int32) + has_below.astype(jnp.int32)
    for j, i in edges:
        @pl.when(inside(w - j, n - i))
        def _():
            pl.semaphore_signal(
                barrier, inc=1, device_id={"wide": w - j, "narrow": n - i}, device_id_type=MESH
            )

        expected = expected + inside(w + j, n + i).astype(jnp.int32)
    pl.semaphore_wait(barrier, expected)

    def edge_copy(which, index, toward=1):
        j, i = edges[index]
        ref = (frames, halo_out)[which]
        if i == 0:
            source, target = pl.ds(1, rows), pl.ds(1, rows)
        elif i == 1:
            source, target = pl.ds(rows, 1), pl.ds(0, 1)
        else:
            source, target = pl.ds(1, 1), pl.ds(rows + 1, 1)
        return pltpu.make_async_remote_copy(
            src_ref=ref.at[2, source],
            dst_ref=ref.at[2 - j, target],
            send_sem=edge_send.at[which, index],
            recv_sem=edge_recv.at[which, index],
            device_id={"wide": w + toward * j, "narrow": n + toward * i},
            device_id_type=MESH,
        )

    def send_edges(which):
        for index, (j, i) in enumerate(edges):
            @pl.when(inside(w + j, n + i))
            def _():
                edge_copy(which, index).start()

    def fill_columns(which):
        for index, (j, i) in enumerate(edges):
            @pl.when(inside(w - j, n - i))
            def _():
                edge_copy(which, index, -1).wait_recv()
        ref = (frames, halo_out)[which]
        place = lax.broadcasted_iota(jnp.int32, (rows + 2, cols, chans), 1)
        place = place.reshape((rows + 2) * cols, chans)
        for a in range(3):
            flat = ref[a].reshape((rows + 2) * cols, chans)
            wider = flat.astype(jnp.float32)
            for e in range(3):
                if e == 0:
                    moved = jnp.where(place == 0, 0.0, pltpu.roll(wider, 1, 0))
                    moved = moved.astype(jnp.bfloat16)
                elif e == 1:
                    moved = flat
                else:
                    moved = pltpu.roll(wider, (rows + 2) * cols - 1, 0)
                    moved = jnp.where(place == cols - 1, 0.0, moved).astype(jnp.bfloat16)
                for b in range(3):
                    tap = 9 * a + 3 * b + e
                    columns[:, tap * chans : (tap + 1) * chans] = moved[
                        b * cols : (b + rows) * cols
                    ]

    def convolve(part):
        outs = wide * shapes[part][0]
        size = 3 * chans
        total[...] = jnp.zeros_like(total)

        def step(index, carry):
            at = pl.ds(pl.multiple_of(index * size, LANE), size)
            total[...] += lax.dot_general(
                columns[:, at],
                full[part][:, :, at].reshape(outs, size),
                (((1,), (1,)), ((), ())),
                preferred_element_type=jnp.float32,
            )
            return carry

        lax.fori_loop(0, 9, step, 0)

    strip_tokens = rows * cols // 4

    def strip_copy(kind):
        strip = {"core": n, "y": n, "relay": n + 2 - 4 * y}[kind]
        index = ("core", "y", "relay").index(kind)
        return pltpu.make_async_remote_copy(
            src_ref=patches.at[strip],
            dst_ref=patches.at[strip],
            send_sem=strip_send.at[index],
            recv_sem=strip_recv.at[index],
            device_id=peer_y if kind == "y" else peer_core,
            device_id_type=MESH,
        )

    def strip_landed(kind):
        strip = {"core": n + 1 - 2 * core, "y": n + 2 - 4 * y, "relay": 3 - n}[kind]
        index = ("core", "y", "relay").index(kind)
        return pltpu.make_async_remote_copy(
            src_ref=patches.at[strip],
            dst_ref=patches.at[strip],
            send_sem=strip_send.at[index],
            recv_sem=strip_recv.at[index],
            device_id=peer_y if kind == "y" else peer_core,
            device_id_type=MESH,
        )

    def first_conv():
        complete(0)
        convolve(0)
        outcome = total[...]
        outcome = outcome / (1.0 + jnp.exp(-outcome))
        halo_out[2, 1 : rows + 1] = outcome.astype(jnp.bfloat16).reshape(rows, cols, chans)
        send_edges(1)

    def second_conv():
        fill_columns(1)
        complete(1)
        convolve(1)
        result = total[...] + latent[0].reshape(rows * cols, chans).astype(jnp.float32)
        for part in range(chans // LANE):
            lanes[part] = result[:, part * LANE : (part + 1) * LANE]
        for b in range(2):
            for e in range(2):
                for part in range(chans // LANE):
                    pieces = [
                        lanes[part, pl.ds((2 * p + b) * cols + e, cols // 2, stride=2), :]
                        for p in range(rows // 2)
                    ]
                    at = (2 * b + e) * chans + part * LANE
                    patches[n, :, at : at + LANE] = jnp.concatenate(pieces, axis=0).astype(
                        jnp.bfloat16
                    )
        strip_copy("core").start()
        strip_copy("y").start()

    def window(part, shard, kind):
        half, third = strips(shapes[part][1])
        start, size = {
            "own": (core * half + y * third, half - third),
            "to_y": (core * half + y * (half - third), third),
            "from_y": (core * half + (1 - y) * (half - third), third),
            "core_own": ((1 - core) * half + y * third, half - third),
            "core_y": ((1 - core) * half + (1 - y) * (half - third), third),
        }[kind]
        cols = pl.ds(pl.multiple_of(start * LANE, LANE), size * LANE)
        return (shard, slice(None), cols)

    def transfer(part, shard, kind, lane, peer, own=False):
        at = window(part, shard, kind)
        target = full[part].at[at]
        source = mine[part].at[at[1:]] if own else target
        arrive = {"own": 0, "to_y": 1, "from_y": 3}[kind]
        if lane == "core" and kind == "own":
            arrive = 2
        send = ("up", "down", "x", "y", "core", "core_y").index(lane if kind != "from_y" else "core_y")
        return pltpu.make_async_remote_copy(
            src_ref=source,
            dst_ref=target,
            send_sem=send_sem.at[part, shard, send],
            recv_sem=recv_sem.at[part, shard, arrive],
            device_id=peer,
            device_id_type=MESH,
        )

    def landed(part, shard, kind):
        at = window(part, shard, kind)
        target = full[part].at[at]
        arrive = {"own": 0, "from_y": 1, "core_own": 2, "core_y": 3}[kind]
        return pltpu.make_async_remote_copy(
            src_ref=target,
            dst_ref=target,
            send_sem=send_sem.at[part, shard, 0],
            recv_sem=recv_sem.at[part, shard, arrive],
            device_id=peer_core,
            device_id_type=MESH,
        )

    def pass_on(part, shard):
        transfer(part, shard, "to_y", "y", peer_y).start()
        transfer(part, shard, "own", "core", peer_core).start()

    def from_partner(part, row):
        shard = 2 * row + 1 - x
        landed(part, shard, "own").wait_recv()
        pass_on(part, shard)

    def from_y(part, shard):
        landed(part, shard, "from_y").wait_recv()
        transfer(part, shard, "from_y", "core", peer_core).start()

    def stage(part, d):
        if d == 0:
            @pl.when(has_above)
            def _():
                transfer(part, w, "own", "up", above, own=True).start()

            @pl.when(has_below)
            def _():
                transfer(part, w, "own", "down", below, own=True).start()

            transfer(part, w, "own", "x", peer_x, own=True).start()
            pltpu.make_async_copy(mine[part], full[part].at[w], own_sem.at[part]).start()
            return

        @pl.when(z >= d)
        def _():
            shard = w - 2 * d
            landed(part, shard, "own").wait_recv()

            @pl.when(has_above)
            def _():
                transfer(part, shard, "own", "up", above).start()

            transfer(part, shard, "own", "x", peer_x).start()
            pass_on(part, shard)

        @pl.when(z + d < depth)
        def _():
            shard = w + 2 * d
            landed(part, shard, "own").wait_recv()

            @pl.when(has_below)
            def _():
                transfer(part, shard, "own", "down", below).start()

            transfer(part, shard, "own", "x", peer_x).start()
            pass_on(part, shard)

        late(part, d - 1)

    def late(part, d):
        for sign in (-1, 1) if d else (1,):
            row = z + sign * d

            @pl.when((row >= 0) & (row < depth))
            def _():
                from_partner(part, row)
        if d >= 1:
            later(part, d - 1)

    def later(part, d):
        for sign in (-1, 1) if d else (1,):
            row = z + sign * d

            @pl.when((row >= 0) & (row < depth))
            def _():
                if d:
                    from_y(part, 2 * row + x)
                from_y(part, 2 * row + 1 - x)

    def complete(part):
        pltpu.make_async_copy(mine[part], full[part].at[w], own_sem.at[part]).wait()
        for shard in range(wide):
            @pl.when(shard != w)
            def _():
                landed(part, shard, "core_own").wait_recv()
                landed(part, shard, "core_y").wait_recv()

    begins = (0, 2, 4)
    for tick in range(begins[-1] + depth + 2):
        for part in range(count):
            d = tick - begins[part]
            if 0 <= d < depth:
                stage(part, d)
            elif d == depth:
                late(part, d - 1)
            elif d == depth + 1:
                later(part, d - 2)
        if tick == 0:
            send_edges(0)
        if tick == 2:
            fill_columns(0)
        if tick == depth + 1:
            first_conv()
        if tick == depth + 3:
            second_conv()
    strip_landed("y").wait_recv()
    strip_copy("relay").start()
    complete(2)
    strip_landed("core").wait_recv()
    strip_landed("relay").wait_recv()
    for kind in ("core", "y", "relay"):
        strip_copy(kind).wait_send()
    for which in range(2):
        for index, (j, i) in enumerate(edges):
            @pl.when(inside(w + j, n + i))
            def _():
                edge_copy(which, index).wait_send()
    for part in range(count):
        for row in range(depth):
            for side in range(2):
                shard = 2 * row + side

                @pl.when(shard != w)
                def _():
                    transfer(part, shard, "to_y", "y", peer_y).wait_send()
                    transfer(part, shard, "own", "core", peer_core).wait_send()
                    transfer(part, shard, "from_y", "core", peer_core).wait_send()

                @pl.when(side == x)
                def _():
                    transfer(part, shard, "own", "x", peer_x).wait_send()

                    @pl.when(has_above & (row <= z))
                    def _():
                        transfer(part, shard, "own", "up", above).wait_send()

                    @pl.when(has_below & (row >= z))
                    def _():
                        transfer(part, shard, "own", "down", below).wait_send()


def conv_block(latent, parts):
    wide, narrow = lax.axis_size("wide"), lax.axis_size("narrow")
    shapes = [part.shape for part in parts]
    count = len(parts)
    rows, cols, chans = latent.shape[1:]
    whole = [(wide,) + shape for shape in shapes]
    return pl.pallas_call(
        functools.partial(block_kernel, wide, narrow, shapes),
        out_shape=[
            jax.ShapeDtypeStruct((narrow, rows * cols // 4, 4 * chans), jnp.bfloat16),
            jax.ShapeDtypeStruct(whole[2], jnp.bfloat16),
        ],
        in_specs=[pl.BlockSpec(memory_space=pltpu.VMEM)]
        + [pl.BlockSpec(memory_space=pltpu.HBM)] * count,
        out_specs=[
            pl.BlockSpec(memory_space=pltpu.VMEM),
            pl.BlockSpec(memory_space=pl.ANY),
        ],
        scratch_shapes=[
            pltpu.VMEM(whole[0], jnp.bfloat16),
            pltpu.VMEM(whole[1], jnp.bfloat16),
            pltpu.VMEM((3, rows + 2, cols, chans), jnp.bfloat16),
            pltpu.VMEM((3, rows + 2, cols, chans), jnp.bfloat16),
            pltpu.VMEM((rows * cols, 27 * chans), jnp.bfloat16),
            pltpu.VMEM((rows * cols, chans), jnp.float32),
            pltpu.VMEM((chans // LANE, rows * cols, LANE), jnp.float32),
            pltpu.SemaphoreType.DMA((count,)),
            pltpu.SemaphoreType.DMA((count, wide, 6)),
            pltpu.SemaphoreType.DMA((count, wide, 4)),
            pltpu.SemaphoreType.DMA((2, 8)),
            pltpu.SemaphoreType.DMA((2, 8)),
            pltpu.SemaphoreType.DMA((3,)),
            pltpu.SemaphoreType.DMA((3,)),
        ],
        compiler_params=pltpu.CompilerParams(
            collective_id=0, has_side_effects=True, vmem_limit_bytes=40 * 1024 * 1024
        ),
    )(latent, *parts)


def mix_kernel(
    wide, size, joint, mixed,
    states, came, prefix, back, local, out_sem, in_sem,
):
    w = lax.axis_index("wide")
    heads, lanes, tokens = local.shape
    piece = states.shape[1]
    spare = lanes - size
    blank = jnp.zeros((spare, tokens), jnp.bfloat16)
    mark = lax.broadcasted_iota(jnp.int32, (spare, tokens), 0) == 0
    ones = jnp.where(mark, 1.0, 0.0).astype(jnp.bfloat16)

    def block(which, head, tail):
        at = (which * heads + head) * size
        return jnp.concatenate([joint[at : at + size], tail], axis=0)

    barrier = pltpu.get_barrier_semaphore()

    def peer(step):
        return lax.rem(w + step, wide)

    for step in range(1, wide):
        pl.semaphore_signal(
            barrier, inc=1, device_id={"wide": peer(step)}, device_id_type=MESH
        )

    for head in range(heads):
        outer = lax.dot_general(
            block(2, head, ones), block(1, head, blank), (((1,), (1,)), ((), ())),
            preferred_element_type=jnp.float32,
        ).astype(jnp.bfloat16)
        for row in range(0, lanes, 16):
            index, at = divmod(head * lanes + row, piece)
            states[index, at : at + 16] = outer[row : row + 16]

    def push(phase, step):
        to = peer(step)
        source, target = ((states, came), (prefix, back))[phase]
        return pltpu.make_async_remote_copy(
            src_ref=source.at[to],
            dst_ref=target.at[w],
            send_sem=out_sem.at[phase, step],
            recv_sem=in_sem.at[phase, step],
            device_id={"wide": to},
            device_id_type=MESH,
        )

    def arrived(phase, step):
        sender = lax.rem(w + wide - step, wide)
        target = (came, back)[phase]
        return pltpu.make_async_remote_copy(
            src_ref=target.at[sender],
            dst_ref=target.at[sender],
            send_sem=out_sem.at[phase, step],
            recv_sem=in_sem.at[phase, step],
            device_id={"wide": sender},
            device_id_type=MESH,
        )

    row_ids = lax.broadcasted_iota(jnp.int32, (tokens, tokens), 0)
    col_ids = lax.broadcasted_iota(jnp.int32, (tokens, tokens), 1)
    spot = lax.broadcasted_iota(jnp.int32, (lanes, tokens), 0)

    def inside_frame(head):
        scores = lax.dot_general(
            block(1, head, blank), block(0, head, blank), (((0,), (0,)), ((), ())),
            preferred_element_type=jnp.float32,
        )
        scores = jnp.where(row_ids <= col_ids, scores, 0.0)
        below = jnp.sum(scores, axis=0, keepdims=True)
        above = jnp.dot(
            block(2, head, blank), scores.astype(jnp.bfloat16), preferred_element_type=jnp.float32
        )
        local[head] = jnp.where(spot == size, below, above)

    pl.semaphore_wait(barrier, wide - 1)
    for step in range(1, wide):
        push(0, step).start()
    came[w] = states[w]
    for head in range(heads // 2):
        inside_frame(head)
    for step in range(1, wide):
        arrived(0, step).wait_recv()
    running = jnp.zeros(states.shape[1:], jnp.float32)
    for frame in range(wide):
        prefix[frame] = running.astype(jnp.bfloat16)
        running = running + came[frame].astype(jnp.float32)
    for step in range(1, wide):
        push(1, step).start()
    back[w] = prefix[w]
    for head in range(heads // 2, heads):
        inside_frame(head)
    for step in range(1, wide):
        arrived(1, step).wait_recv()
    for head in range(heads):
        parts = []
        for row in range(0, lanes, 16):
            index, at = divmod(head * lanes + row, piece)
            parts.append(back[index, at : at + 16])
        carried = jnp.dot(
            jnp.concatenate(parts, axis=0), block(0, head, blank),
            preferred_element_type=jnp.float32,
        )
        whole = local[head] + carried
        mixed[head * size : (head + 1) * size] = (
            whole[:size] / whole[size : size + 1]
        ).astype(jnp.bfloat16)
    for phase in range(2):
        for step in range(1, wide):
            push(phase, step).wait_send()


def mix_frames(joint, size):
    wide = lax.axis_size("wide")
    heads, tokens = joint.shape[0] // 3 // size, joint.shape[1]
    pieces = (wide, heads * LANE // wide, LANE)
    return pl.pallas_call(
        functools.partial(mix_kernel, wide, size),
        out_shape=jax.ShapeDtypeStruct((heads * size, tokens), jnp.bfloat16),
        in_specs=[pl.BlockSpec(memory_space=pltpu.VMEM)],
        out_specs=pl.BlockSpec(memory_space=pltpu.VMEM),
        scratch_shapes=[
            pltpu.VMEM(pieces, jnp.bfloat16),
            pltpu.VMEM(pieces, jnp.bfloat16),
            pltpu.VMEM(pieces, jnp.bfloat16),
            pltpu.VMEM(pieces, jnp.bfloat16),
            pltpu.VMEM((heads, LANE, tokens), jnp.float32),
            pltpu.SemaphoreType.DMA((2, wide)),
            pltpu.SemaphoreType.DMA((2, wide)),
        ],
        compiler_params=pltpu.CompilerParams(
            collective_id=1, has_side_effects=True, vmem_limit_bytes=32 * 1024 * 1024
        ),
    )(joint)


def shifted(x, axis, by):
    size = lax.axis_size(axis)
    pairs = [(i, i + by) for i in range(size) if 0 <= i + by < size]
    return lax.ppermute(x, axis, pairs)


def extended(block, sides, width):
    for axis, dim in sides:
        count = lax.axis_size(axis)
        forward = [(i, i + 1) for i in range(count - 1)]
        backward = [(target, source) for source, target in forward]
        low = lax.ppermute(
            lax.slice_in_dim(block, block.shape[dim] - width, None, axis=dim), axis, forward
        )
        high = lax.ppermute(lax.slice_in_dim(block, 0, width, axis=dim), axis, backward)
        block = jnp.concatenate([low, block, high], axis=dim)
    return block


def causal_conv(current, weight):
    before = shifted(current, "wide", 1)
    earlier = shifted(current, "wide", 2)
    stacked = jnp.concatenate([earlier, before, current], axis=0)
    rimmed = extended(stacked, (("narrow", 1),), 1)
    padded = jnp.pad(rimmed, ((0, 0), (0, 0), (1, 1), (0, 0)))
    row_count = current.shape[1]
    col_count = current.shape[2]
    chan_count = current.shape[3]
    block_cols = lax.all_gather(weight, "wide", axis=1, tiled=True)
    summed = jnp.zeros((row_count * col_count, block_cols.shape[1]), jnp.float32)
    for kernel_tap in range(27):
        time_step = kernel_tap // 9
        row_step = kernel_tap // 3 % 3
        col_step = kernel_tap % 3
        window = padded[time_step, row_step : row_step + row_count, col_step : col_step + col_count]
        window = window.reshape(row_count * col_count, chan_count)
        summed = summed + jnp.dot(
            window,
            block_cols[kernel_tap * chan_count : (kernel_tap + 1) * chan_count],
            preferred_element_type=jnp.float32,
        )
    return summed


def embed_tokens(patch_feats, embed_weight):
    return jnp.dot(
        patch_feats,
        lax.all_gather(embed_weight, "wide", axis=1, tiled=True),
        preferred_element_type=jnp.float32,
    ).astype(jnp.bfloat16)


def embedded_plain(latent, conv_first, conv_second, embed_weight):
    row_count = latent.shape[1]
    col_count = latent.shape[2]
    chan_count = latent.shape[3]
    first = causal_conv(latent, conv_first)
    activated = jax.nn.silu(first).astype(jnp.bfloat16).reshape(latent.shape)
    second = causal_conv(activated, conv_second) + latent.reshape(-1, chan_count).astype(
        jnp.float32
    )
    block_out = second.astype(jnp.bfloat16)
    patches = block_out.reshape(row_count // 2, 2, col_count // 2, 2, chan_count)
    patches = patches.transpose(0, 2, 1, 3, 4).reshape(-1, 4 * chan_count)
    return lax.all_gather(embed_tokens(patches, embed_weight), "narrow", axis=0, tiled=True)


def embedded_fused(latent, conv_first, conv_second, embed_weight):
    patches, weights = conv_block(latent, [conv_first.T, conv_second.T, embed_weight.T])
    return lax.dot_general(
        patches.reshape(-1, patches.shape[2]),
        weights.reshape(-1, weights.shape[2]),
        (((1,), (1,)), ((), ())),
        preferred_element_type=jnp.float32,
    ).astype(jnp.bfloat16)


def per_device(latent, conv_first, conv_second, embed_weight, qkv_weight):
    wide, narrow = lax.axis_size("wide"), lax.axis_size("narrow")
    fits = narrow == 4 and wide % 2 == 0 and conv_first.shape[1] % 16 == 0
    embed = embedded_fused if fits else embedded_plain
    embedded = embed(latent, conv_first, conv_second, embed_weight)
    heads_here = qkv_weight.shape[2] // HEAD_DIM
    token_count = embedded.shape[0]
    if heads_here * LANE % (wide * 16) == 0:
        turned = qkv_weight.transpose(0, 2, 1).reshape(-1, qkv_weight.shape[1])
        joint = lax.dot_general(
            turned,
            lax.optimization_barrier(embedded),
            (((1,), (1,)), ((), ())),
            preferred_element_type=jnp.float32,
        )
        row = lax.broadcasted_iota(jnp.int32, joint.shape, 0)
        joint = jnp.where(row < 2 * qkv_weight.shape[2], jax.nn.elu(joint) + 1.0, joint)
        return mix_frames(joint.astype(jnp.bfloat16), HEAD_DIM).T
    query_raw = jnp.dot(embedded, qkv_weight[0], preferred_element_type=jnp.float32)
    key_raw = jnp.dot(embedded, qkv_weight[1], preferred_element_type=jnp.float32)
    val_rows = jnp.dot(embedded, qkv_weight[2], preferred_element_type=jnp.float32).astype(
        jnp.bfloat16
    )
    query_feat = (
        (jax.nn.elu(query_raw) + 1.0)
        .astype(jnp.bfloat16)
        .reshape(token_count, heads_here, HEAD_DIM)
    )
    key_feat = (
        (jax.nn.elu(key_raw) + 1.0).astype(jnp.bfloat16).reshape(token_count, heads_here, HEAD_DIM)
    )
    val_heads = val_rows.reshape(token_count, heads_here, HEAD_DIM)
    scores = jnp.einsum("thd,shd->hts", query_feat, key_feat, preferred_element_type=jnp.float32)
    row_ids = lax.broadcasted_iota(jnp.int32, (token_count, token_count), 0)
    col_ids = lax.broadcasted_iota(jnp.int32, (token_count, token_count), 1)
    scores = jnp.where((col_ids <= row_ids)[None], scores, 0.0)
    local_den = jnp.sum(scores, axis=-1)
    local_num = jnp.einsum(
        "hts,she->the", scores.astype(jnp.bfloat16), val_heads, preferred_element_type=jnp.float32
    )
    state_local = jnp.einsum(
        "thd,the->hde", key_feat, val_heads, preferred_element_type=jnp.float32
    )
    key_local = jnp.sum(key_feat, axis=0, dtype=jnp.float32)
    flat_state = jnp.concatenate([state_local.reshape(-1), key_local.reshape(-1)])
    length_all = flat_state.shape[0]
    peer_count = lax.axis_size("wide")
    per_peer = -(-length_all // peer_count)
    piece_grid = jnp.pad(flat_state, (0, per_peer * peer_count - length_all)).reshape(
        peer_count, per_peer
    )
    lower_ones = (
        lax.broadcasted_iota(jnp.int32, (peer_count, peer_count), 1)
        < lax.broadcasted_iota(jnp.int32, (peer_count, peer_count), 0)
    ).astype(jnp.float32)
    partial_sums = jnp.dot(
        lower_ones,
        lax.all_to_all(
            piece_grid.astype(jnp.bfloat16), "wide", split_axis=0, concat_axis=0, tiled=True
        ).astype(piece_grid.dtype),
        precision=lax.Precision.HIGHEST,
    )
    spread = lax.all_to_all(
        partial_sums.astype(jnp.bfloat16), "wide", split_axis=0, concat_axis=0, tiled=True
    ).astype(partial_sums.dtype)
    flat_prefix = spread.reshape(-1)[:length_all]
    state_size = state_local.size
    state_prev = flat_prefix[:state_size].reshape(state_local.shape)
    key_prev = flat_prefix[state_size:].reshape(key_local.shape)
    query_wide = query_feat.astype(jnp.float32)
    carried_num = jnp.einsum(
        "thd,hde->the", query_wide, state_prev, precision=lax.Precision.HIGHEST
    )
    carried_den = jnp.einsum("thd,hd->th", query_wide, key_prev, precision=lax.Precision.HIGHEST)
    result = (local_num + carried_num) / (local_den.T + carried_den)[..., None]
    return result.astype(jnp.bfloat16).reshape(token_count, heads_here * HEAD_DIM)


def solution(mesh):
    return jax.shard_map(
        per_device,
        mesh=mesh,
        in_specs=(
            P("wide", "narrow", None, None),
            P(None, "wide"),
            P(None, "wide"),
            P(None, "wide"),
            P(None, None, "narrow"),
        ),
        out_specs=P("wide", "narrow"),
        check_vma=False,
    )
```

```python
import functools

import jax
import jax.numpy as jnp
from jax import lax
from jax.experimental import pallas as pl
from jax.experimental.pallas import tpu as pltpu
from jax.sharding import PartitionSpec as P

HEAD_DIM = 112
LANE = 128
MESH = pl.DeviceIdType.MESH


def strips(lanes):
    half = lanes // LANE // 2
    return half, max(1, half * 41 // 100)


def block_kernel(
    wide, narrow, shapes, latent, first_w, second_w, embed_w, patches, embed_full,
    first_full, second_full, frames, halo_out, columns, total, lanes, own_sem, send_sem, recv_sem,
    edge_send, edge_recv, strip_send, strip_recv,
):
    count = len(shapes)
    mine = (first_w, second_w, embed_w)
    full = (first_full, second_full, embed_full)
    rows, cols, chans = latent.shape[1:]
    frames[...] = jnp.zeros_like(frames)
    halo_out[...] = jnp.zeros_like(halo_out)
    frames[2, 1 : rows + 1] = latent[0]
    w = lax.axis_index("wide")
    n = lax.axis_index("narrow")
    z, x = w // 2, lax.rem(w, 2)
    y, core = lax.rem(n // 2, 2), lax.rem(n, 2)
    depth = wide // 2
    peer_x = {"wide": w + 1 - 2 * x}
    peer_y = {"narrow": n + 2 - 4 * y}
    peer_core = {"narrow": n + 1 - 2 * core}
    above, below = {"wide": w + 2}, {"wide": w - 2}
    has_above, has_below = z < depth - 1, z > 0

    barrier = pltpu.get_barrier_semaphore()
    for peer in (peer_x, peer_y, peer_core):
        pl.semaphore_signal(barrier, inc=1, device_id=peer, device_id_type=MESH)

    @pl.when(has_above)
    def _():
        pl.semaphore_signal(barrier, inc=1, device_id=above, device_id_type=MESH)

    @pl.when(has_below)
    def _():
        pl.semaphore_signal(barrier, inc=1, device_id=below, device_id_type=MESH)

    def inside(frame, strip):
        return (frame >= 0) & (frame < wide) & (strip >= 0) & (strip < narrow)

    edges = [(j, i) for j in (2, 1, 0) for i in (0, -1, 1) if (j, i) != (0, 0)]
    expected = 3 + has_above.astype(jnp.int32) + has_below.astype(jnp.int32)
    for j, i in edges:
        @pl.when(inside(w - j, n - i))
        def _():
            pl.semaphore_signal(
                barrier, inc=1, device_id={"wide": w - j, "narrow": n - i}, device_id_type=MESH
            )

        expected = expected + inside(w + j, n + i).astype(jnp.int32)
    pl.semaphore_wait(barrier, expected)

    def edge_copy(which, index, toward=1):
        j, i = edges[index]
        ref = (frames, halo_out)[which]
        if i == 0:
            source, target = pl.ds(1, rows), pl.ds(1, rows)
        elif i == 1:
            source, target = pl.ds(rows, 1), pl.ds(0, 1)
        else:
            source, target = pl.ds(1, 1), pl.ds(rows + 1, 1)
        return pltpu.make_async_remote_copy(
            src_ref=ref.at[2, source],
            dst_ref=ref.at[2 - j, target],
            send_sem=edge_send.at[which, index],
            recv_sem=edge_recv.at[which, index],
            device_id={"wide": w + toward * j, "narrow": n + toward * i},
            device_id_type=MESH,
        )

    def send_edges(which):
        for index, (j, i) in enumerate(edges):
            @pl.when(inside(w + j, n + i))
            def _():
                edge_copy(which, index).start()

    def fill_columns(which):
        for index, (j, i) in enumerate(edges):
            @pl.when(inside(w - j, n - i))
            def _():
                edge_copy(which, index, -1).wait_recv()
        ref = (frames, halo_out)[which]
        place = lax.broadcasted_iota(jnp.int32, (rows + 2, cols, chans), 1)
        place = place.reshape((rows + 2) * cols, chans)
        for a in range(3):
            flat = ref[a].reshape((rows + 2) * cols, chans)
            wider = flat.astype(jnp.float32)
            for e in range(3):
                if e == 0:
                    moved = jnp.where(place == 0, 0.0, pltpu.roll(wider, 1, 0))
                    moved = moved.astype(jnp.bfloat16)
                elif e == 1:
                    moved = flat
                else:
                    moved = pltpu.roll(wider, (rows + 2) * cols - 1, 0)
                    moved = jnp.where(place == cols - 1, 0.0, moved).astype(jnp.bfloat16)
                for b in range(3):
                    tap = 9 * a + 3 * b + e
                    columns[:, tap * chans : (tap + 1) * chans] = moved[
                        b * cols : (b + rows) * cols
                    ]

    def convolve(part):
        outs = wide * shapes[part][0]
        size = 3 * chans
        total[...] = jnp.zeros_like(total)

        def step(index, carry):
            at = pl.ds(pl.multiple_of(index * size, LANE), size)
            total[...] += lax.dot_general(
                columns[:, at],
                full[part][:, :, at].reshape(outs, size),
                (((1,), (1,)), ((), ())),
                preferred_element_type=jnp.float32,
            )
            return carry

        lax.fori_loop(0, 9, step, 0)

    strip_tokens = rows * cols // 4

    def strip_copy(kind):
        strip = {"core": n, "y": n, "relay": n + 2 - 4 * y}[kind]
        index = ("core", "y", "relay").index(kind)
        return pltpu.make_async_remote_copy(
            src_ref=patches.at[strip],
            dst_ref=patches.at[strip],
            send_sem=strip_send.at[index],
            recv_sem=strip_recv.at[index],
            device_id=peer_y if kind == "y" else peer_core,
            device_id_type=MESH,
        )

    def strip_landed(kind):
        strip = {"core": n + 1 - 2 * core, "y": n + 2 - 4 * y, "relay": 3 - n}[kind]
        index = ("core", "y", "relay").index(kind)
        return pltpu.make_async_remote_copy(
            src_ref=patches.at[strip],
            dst_ref=patches.at[strip],
            send_sem=strip_send.at[index],
            recv_sem=strip_recv.at[index],
            device_id=peer_y if kind == "y" else peer_core,
            device_id_type=MESH,
        )

    def first_conv():
        complete(0)
        convolve(0)
        outcome = total[...]
        outcome = outcome / (1.0 + jnp.exp(-outcome))
        halo_out[2, 1 : rows + 1] = outcome.astype(jnp.bfloat16).reshape(rows, cols, chans)
        send_edges(1)

    def second_conv():
        fill_columns(1)
        complete(1)
        convolve(1)
        result = total[...] + latent[0].reshape(rows * cols, chans).astype(jnp.float32)
        for part in range(chans // LANE):
            lanes[part] = result[:, part * LANE : (part + 1) * LANE]
        for b in range(2):
            for e in range(2):
                for part in range(chans // LANE):
                    pieces = [
                        lanes[part, pl.ds((2 * p + b) * cols + e, cols // 2, stride=2), :]
                        for p in range(rows // 2)
                    ]
                    at = (2 * b + e) * chans + part * LANE
                    patches[n, :, at : at + LANE] = jnp.concatenate(pieces, axis=0).astype(
                        jnp.bfloat16
                    )
        strip_copy("core").start()
        strip_copy("y").start()

    def window(part, shard, kind):
        half, third = strips(shapes[part][1])
        start, size = {
            "own": (core * half + y * third, half - third),
            "to_y": (core * half + y * (half - third), third),
            "from_y": (core * half + (1 - y) * (half - third), third),
            "core_own": ((1 - core) * half + y * third, half - third),
            "core_y": ((1 - core) * half + (1 - y) * (half - third), third),
        }[kind]
        cols = pl.ds(pl.multiple_of(start * LANE, LANE), size * LANE)
        return (shard, slice(None), cols)

    def transfer(part, shard, kind, lane, peer, own=False):
        at = window(part, shard, kind)
        target = full[part].at[at]
        source = mine[part].at[at[1:]] if own else target
        arrive = {"own": 0, "to_y": 1, "from_y": 3}[kind]
        if lane == "core" and kind == "own":
            arrive = 2
        send = ("up", "down", "x", "y", "core", "core_y").index(lane if kind != "from_y" else "core_y")
        return pltpu.make_async_remote_copy(
            src_ref=source,
            dst_ref=target,
            send_sem=send_sem.at[part, shard, send],
            recv_sem=recv_sem.at[part, shard, arrive],
            device_id=peer,
            device_id_type=MESH,
        )

    def landed(part, shard, kind):
        at = window(part, shard, kind)
        target = full[part].at[at]
        arrive = {"own": 0, "from_y": 1, "core_own": 2, "core_y": 3}[kind]
        return pltpu.make_async_remote_copy(
            src_ref=target,
            dst_ref=target,
            send_sem=send_sem.at[part, shard, 0],
            recv_sem=recv_sem.at[part, shard, arrive],
            device_id=peer_core,
            device_id_type=MESH,
        )

    def pass_on(part, shard):
        transfer(part, shard, "to_y", "y", peer_y).start()
        transfer(part, shard, "own", "core", peer_core).start()

    def from_partner(part, row):
        shard = 2 * row + 1 - x
        landed(part, shard, "own").wait_recv()
        pass_on(part, shard)

    def from_y(part, shard):
        landed(part, shard, "from_y").wait_recv()
        transfer(part, shard, "from_y", "core", peer_core).start()

    def stage(part, d):
        if d == 0:
            @pl.when(has_above)
            def _():
                transfer(part, w, "own", "up", above, own=True).start()

            @pl.when(has_below)
            def _():
                transfer(part, w, "own", "down", below, own=True).start()

            transfer(part, w, "own", "x", peer_x, own=True).start()
            pltpu.make_async_copy(mine[part], full[part].at[w], own_sem.at[part]).start()
            return

        @pl.when(z >= d)
        def _():
            shard = w - 2 * d
            landed(part, shard, "own").wait_recv()

            @pl.when(has_above)
            def _():
                transfer(part, shard, "own", "up", above).start()

            transfer(part, shard, "own", "x", peer_x).start()
            pass_on(part, shard)

        @pl.when(z + d < depth)
        def _():
            shard = w + 2 * d
            landed(part, shard, "own").wait_recv()

            @pl.when(has_below)
            def _():
                transfer(part, shard, "own", "down", below).start()

            transfer(part, shard, "own", "x", peer_x).start()
            pass_on(part, shard)

        late(part, d - 1)

    def late(part, d):
        for sign in (-1, 1) if d else (1,):
            row = z + sign * d

            @pl.when((row >= 0) & (row < depth))
            def _():
                from_partner(part, row)
        if d >= 1:
            later(part, d - 1)

    def later(part, d):
        for sign in (-1, 1) if d else (1,):
            row = z + sign * d

            @pl.when((row >= 0) & (row < depth))
            def _():
                if d:
                    from_y(part, 2 * row + x)
                from_y(part, 2 * row + 1 - x)

    def complete(part):
        pltpu.make_async_copy(mine[part], full[part].at[w], own_sem.at[part]).wait()
        for shard in range(wide):
            @pl.when(shard != w)
            def _():
                landed(part, shard, "core_own").wait_recv()
                landed(part, shard, "core_y").wait_recv()

    begins = (0, 2, 4)
    for tick in range(begins[-1] + depth + 2):
        for part in range(count):
            d = tick - begins[part]
            if 0 <= d < depth:
                stage(part, d)
            elif d == depth:
                late(part, d - 1)
            elif d == depth + 1:
                later(part, d - 2)
        if tick == 0:
            send_edges(0)
        if tick == 2:
            fill_columns(0)
        if tick == depth + 1:
            first_conv()
        if tick == depth + 3:
            second_conv()
    strip_landed("y").wait_recv()
    strip_copy("relay").start()
    complete(2)
    strip_landed("core").wait_recv()
    strip_landed("relay").wait_recv()
    for kind in ("core", "y", "relay"):
        strip_copy(kind).wait_send()
    for which in range(2):
        for index, (j, i) in enumerate(edges):
            @pl.when(inside(w + j, n + i))
            def _():
                edge_copy(which, index).wait_send()
    for part in range(count):
        for row in range(depth):
            for side in range(2):
                shard = 2 * row + side

                @pl.when(shard != w)
                def _():
                    transfer(part, shard, "to_y", "y", peer_y).wait_send()
                    transfer(part, shard, "own", "core", peer_core).wait_send()
                    transfer(part, shard, "from_y", "core", peer_core).wait_send()

                @pl.when(side == x)
                def _():
                    transfer(part, shard, "own", "x", peer_x).wait_send()

                    @pl.when(has_above & (row <= z))
                    def _():
                        transfer(part, shard, "own", "up", above).wait_send()

                    @pl.when(has_below & (row >= z))
                    def _():
                        transfer(part, shard, "own", "down", below).wait_send()


def conv_block(latent, parts):
    wide, narrow = lax.axis_size("wide"), lax.axis_size("narrow")
    shapes = [part.shape for part in parts]
    count = len(parts)
    rows, cols, chans = latent.shape[1:]
    whole = [(wide,) + shape for shape in shapes]
    return pl.pallas_call(
        functools.partial(block_kernel, wide, narrow, shapes),
        out_shape=[
            jax.ShapeDtypeStruct((narrow, rows * cols // 4, 4 * chans), jnp.bfloat16),
            jax.ShapeDtypeStruct(whole[2], jnp.bfloat16),
        ],
        in_specs=[pl.BlockSpec(memory_space=pltpu.VMEM)]
        + [pl.BlockSpec(memory_space=pltpu.HBM)] * count,
        out_specs=[
            pl.BlockSpec(memory_space=pltpu.VMEM),
            pl.BlockSpec(memory_space=pl.ANY),
        ],
        scratch_shapes=[
            pltpu.VMEM(whole[0], jnp.bfloat16),
            pltpu.VMEM(whole[1], jnp.bfloat16),
            pltpu.VMEM((3, rows + 2, cols, chans), jnp.bfloat16),
            pltpu.VMEM((3, rows + 2, cols, chans), jnp.bfloat16),
            pltpu.VMEM((rows * cols, 27 * chans), jnp.bfloat16),
            pltpu.VMEM((rows * cols, chans), jnp.float32),
            pltpu.VMEM((chans // LANE, rows * cols, LANE), jnp.float32),
            pltpu.SemaphoreType.DMA((count,)),
            pltpu.SemaphoreType.DMA((count, wide, 6)),
            pltpu.SemaphoreType.DMA((count, wide, 4)),
            pltpu.SemaphoreType.DMA((2, 8)),
            pltpu.SemaphoreType.DMA((2, 8)),
            pltpu.SemaphoreType.DMA((3,)),
            pltpu.SemaphoreType.DMA((3,)),
        ],
        compiler_params=pltpu.CompilerParams(
            collective_id=0, has_side_effects=True, vmem_limit_bytes=56 * 1024 * 1024
        ),
    )(latent, *parts)


def mix_kernel(
    wide, size, joint, mixed,
    states, came, prefix, back, local, out_sem, in_sem,
):
    w = lax.axis_index("wide")
    heads, lanes, tokens = local.shape
    piece = states.shape[1]
    spare = lanes - size
    blank = jnp.zeros((spare, tokens), jnp.bfloat16)
    mark = lax.broadcasted_iota(jnp.int32, (spare, tokens), 0) == 0
    ones = jnp.where(mark, 1.0, 0.0).astype(jnp.bfloat16)

    def block(which, head, tail):
        at = (which * heads + head) * size
        return jnp.concatenate([joint[at : at + size], tail], axis=0)

    barrier = pltpu.get_barrier_semaphore()

    def peer(step):
        return lax.rem(w + step, wide)

    for step in range(1, wide):
        pl.semaphore_signal(
            barrier, inc=1, device_id={"wide": peer(step)}, device_id_type=MESH
        )

    for head in range(heads):
        outer = lax.dot_general(
            block(2, head, ones), block(1, head, blank), (((1,), (1,)), ((), ())),
            preferred_element_type=jnp.float32,
        ).astype(jnp.bfloat16)
        for row in range(0, lanes, 16):
            index, at = divmod(head * lanes + row, piece)
            states[index, at : at + 16] = outer[row : row + 16]

    def push(phase, step):
        to = peer(step)
        source, target = ((states, came), (prefix, back))[phase]
        return pltpu.make_async_remote_copy(
            src_ref=source.at[to],
            dst_ref=target.at[w],
            send_sem=out_sem.at[phase, step],
            recv_sem=in_sem.at[phase, step],
            device_id={"wide": to},
            device_id_type=MESH,
        )

    def arrived(phase, step):
        sender = lax.rem(w + wide - step, wide)
        target = (came, back)[phase]
        return pltpu.make_async_remote_copy(
            src_ref=target.at[sender],
            dst_ref=target.at[sender],
            send_sem=out_sem.at[phase, step],
            recv_sem=in_sem.at[phase, step],
            device_id={"wide": sender},
            device_id_type=MESH,
        )

    row_ids = lax.broadcasted_iota(jnp.int32, (tokens, tokens), 0)
    col_ids = lax.broadcasted_iota(jnp.int32, (tokens, tokens), 1)
    spot = lax.broadcasted_iota(jnp.int32, (lanes, tokens), 0)

    def inside_frame(head):
        scores = lax.dot_general(
            block(1, head, blank), block(0, head, blank), (((0,), (0,)), ((), ())),
            preferred_element_type=jnp.float32,
        )
        scores = jnp.where(row_ids <= col_ids, scores, 0.0)
        below = jnp.sum(scores, axis=0, keepdims=True)
        above = jnp.dot(
            block(2, head, blank), scores.astype(jnp.bfloat16), preferred_element_type=jnp.float32
        )
        local[head] = jnp.where(spot == size, below, above)

    pl.semaphore_wait(barrier, wide - 1)
    for step in range(1, wide):
        push(0, step).start()
    came[w] = states[w]
    for head in range(heads // 2):
        inside_frame(head)
    for step in range(1, wide):
        arrived(0, step).wait_recv()
    running = jnp.zeros(states.shape[1:], jnp.float32)
    for frame in range(wide):
        prefix[frame] = running.astype(jnp.bfloat16)
        running = running + came[frame].astype(jnp.float32)
    for step in range(1, wide):
        push(1, step).start()
    back[w] = prefix[w]
    for head in range(heads // 2, heads):
        inside_frame(head)
    for step in range(1, wide):
        arrived(1, step).wait_recv()
    for head in range(heads):
        parts = []
        for row in range(0, lanes, 16):
            index, at = divmod(head * lanes + row, piece)
            parts.append(back[index, at : at + 16])
        carried = jnp.dot(
            jnp.concatenate(parts, axis=0), block(0, head, blank),
            preferred_element_type=jnp.float32,
        )
        whole = local[head] + carried
        mixed[head * size : (head + 1) * size] = (
            whole[:size] / whole[size : size + 1]
        ).astype(jnp.bfloat16)
    for phase in range(2):
        for step in range(1, wide):
            push(phase, step).wait_send()


def mix_frames(joint, size):
    wide = lax.axis_size("wide")
    heads, tokens = joint.shape[0] // 3 // size, joint.shape[1]
    pieces = (wide, heads * LANE // wide, LANE)
    return pl.pallas_call(
        functools.partial(mix_kernel, wide, size),
        out_shape=jax.ShapeDtypeStruct((heads * size, tokens), jnp.bfloat16),
        in_specs=[pl.BlockSpec(memory_space=pltpu.VMEM)],
        out_specs=pl.BlockSpec(memory_space=pltpu.VMEM),
        scratch_shapes=[
            pltpu.VMEM(pieces, jnp.bfloat16),
            pltpu.VMEM(pieces, jnp.bfloat16),
            pltpu.VMEM(pieces, jnp.bfloat16),
            pltpu.VMEM(pieces, jnp.bfloat16),
            pltpu.VMEM((heads, LANE, tokens), jnp.float32),
            pltpu.SemaphoreType.DMA((2, wide)),
            pltpu.SemaphoreType.DMA((2, wide)),
        ],
        compiler_params=pltpu.CompilerParams(
            collective_id=1, has_side_effects=True, vmem_limit_bytes=32 * 1024 * 1024
        ),
    )(joint)


def shifted(x, axis, by):
    size = lax.axis_size(axis)
    pairs = [(i, i + by) for i in range(size) if 0 <= i + by < size]
    return lax.ppermute(x, axis, pairs)


def extended(block, sides, width):
    for axis, dim in sides:
        count = lax.axis_size(axis)
        forward = [(i, i + 1) for i in range(count - 1)]
        backward = [(target, source) for source, target in forward]
        low = lax.ppermute(
            lax.slice_in_dim(block, block.shape[dim] - width, None, axis=dim), axis, forward
        )
        high = lax.ppermute(lax.slice_in_dim(block, 0, width, axis=dim), axis, backward)
        block = jnp.concatenate([low, block, high], axis=dim)
    return block


def causal_conv(current, weight):
    before = shifted(current, "wide", 1)
    earlier = shifted(current, "wide", 2)
    stacked = jnp.concatenate([earlier, before, current], axis=0)
    rimmed = extended(stacked, (("narrow", 1),), 1)
    padded = jnp.pad(rimmed, ((0, 0), (0, 0), (1, 1), (0, 0)))
    row_count = current.shape[1]
    col_count = current.shape[2]
    chan_count = current.shape[3]
    block_cols = lax.all_gather(weight, "wide", axis=1, tiled=True)
    summed = jnp.zeros((row_count * col_count, block_cols.shape[1]), jnp.float32)
    for kernel_tap in range(27):
        time_step = kernel_tap // 9
        row_step = kernel_tap // 3 % 3
        col_step = kernel_tap % 3
        window = padded[time_step, row_step : row_step + row_count, col_step : col_step + col_count]
        window = window.reshape(row_count * col_count, chan_count)
        summed = summed + jnp.dot(
            window,
            block_cols[kernel_tap * chan_count : (kernel_tap + 1) * chan_count],
            preferred_element_type=jnp.float32,
        )
    return summed


def embed_tokens(patch_feats, embed_weight):
    return jnp.dot(
        patch_feats,
        lax.all_gather(embed_weight, "wide", axis=1, tiled=True),
        preferred_element_type=jnp.float32,
    ).astype(jnp.bfloat16)


def embedded_plain(latent, conv_first, conv_second, embed_weight):
    row_count = latent.shape[1]
    col_count = latent.shape[2]
    chan_count = latent.shape[3]
    first = causal_conv(latent, conv_first)
    activated = jax.nn.silu(first).astype(jnp.bfloat16).reshape(latent.shape)
    second = causal_conv(activated, conv_second) + latent.reshape(-1, chan_count).astype(
        jnp.float32
    )
    block_out = second.astype(jnp.bfloat16)
    patches = block_out.reshape(row_count // 2, 2, col_count // 2, 2, chan_count)
    patches = patches.transpose(0, 2, 1, 3, 4).reshape(-1, 4 * chan_count)
    return lax.all_gather(embed_tokens(patches, embed_weight), "narrow", axis=0, tiled=True)


def embedded_fused(latent, conv_first, conv_second, embed_weight):
    patches, weights = conv_block(latent, [conv_first.T, conv_second.T, embed_weight.T])
    return lax.dot_general(
        patches.reshape(-1, patches.shape[2]),
        weights.reshape(-1, weights.shape[2]),
        (((1,), (1,)), ((), ())),
        preferred_element_type=jnp.float32,
    ).astype(jnp.bfloat16)


def per_device(latent, conv_first, conv_second, embed_weight, qkv_weight):
    wide, narrow = lax.axis_size("wide"), lax.axis_size("narrow")
    fits = narrow == 4 and wide % 2 == 0 and conv_first.shape[1] % 16 == 0
    embed = embedded_fused if fits else embedded_plain
    embedded = embed(latent, conv_first, conv_second, embed_weight)
    heads_here = qkv_weight.shape[2] // HEAD_DIM
    token_count = embedded.shape[0]
    if heads_here * LANE % (wide * 16) == 0:
        turned = qkv_weight.transpose(0, 2, 1).reshape(-1, qkv_weight.shape[1])
        joint = lax.dot_general(
            turned,
            lax.optimization_barrier(embedded),
            (((1,), (1,)), ((), ())),
            preferred_element_type=jnp.float32,
        )
        row = lax.broadcasted_iota(jnp.int32, joint.shape, 0)
        joint = jnp.where(row < 2 * qkv_weight.shape[2], jax.nn.elu(joint) + 1.0, joint)
        return mix_frames(joint.astype(jnp.bfloat16), HEAD_DIM).T
    query_raw = jnp.dot(embedded, qkv_weight[0], preferred_element_type=jnp.float32)
    key_raw = jnp.dot(embedded, qkv_weight[1], preferred_element_type=jnp.float32)
    val_rows = jnp.dot(embedded, qkv_weight[2], preferred_element_type=jnp.float32).astype(
        jnp.bfloat16
    )
    query_feat = (
        (jax.nn.elu(query_raw) + 1.0)
        .astype(jnp.bfloat16)
        .reshape(token_count, heads_here, HEAD_DIM)
    )
    key_feat = (
        (jax.nn.elu(key_raw) + 1.0).astype(jnp.bfloat16).reshape(token_count, heads_here, HEAD_DIM)
    )
    val_heads = val_rows.reshape(token_count, heads_here, HEAD_DIM)
    scores = jnp.einsum("thd,shd->hts", query_feat, key_feat, preferred_element_type=jnp.float32)
    row_ids = lax.broadcasted_iota(jnp.int32, (token_count, token_count), 0)
    col_ids = lax.broadcasted_iota(jnp.int32, (token_count, token_count), 1)
    scores = jnp.where((col_ids <= row_ids)[None], scores, 0.0)
    local_den = jnp.sum(scores, axis=-1)
    local_num = jnp.einsum(
        "hts,she->the", scores.astype(jnp.bfloat16), val_heads, preferred_element_type=jnp.float32
    )
    state_local = jnp.einsum(
        "thd,the->hde", key_feat, val_heads, preferred_element_type=jnp.float32
    )
    key_local = jnp.sum(key_feat, axis=0, dtype=jnp.float32)
    flat_state = jnp.concatenate([state_local.reshape(-1), key_local.reshape(-1)])
    length_all = flat_state.shape[0]
    peer_count = lax.axis_size("wide")
    per_peer = -(-length_all // peer_count)
    piece_grid = jnp.pad(flat_state, (0, per_peer * peer_count - length_all)).reshape(
        peer_count, per_peer
    )
    lower_ones = (
        lax.broadcasted_iota(jnp.int32, (peer_count, peer_count), 1)
        < lax.broadcasted_iota(jnp.int32, (peer_count, peer_count), 0)
    ).astype(jnp.float32)
    partial_sums = jnp.dot(
        lower_ones,
        lax.all_to_all(
            piece_grid.astype(jnp.bfloat16), "wide", split_axis=0, concat_axis=0, tiled=True
        ).astype(piece_grid.dtype),
        precision=lax.Precision.HIGHEST,
    )
    spread = lax.all_to_all(
        partial_sums.astype(jnp.bfloat16), "wide", split_axis=0, concat_axis=0, tiled=True
    ).astype(partial_sums.dtype)
    flat_prefix = spread.reshape(-1)[:length_all]
    state_size = state_local.size
    state_prev = flat_prefix[:state_size].reshape(state_local.shape)
    key_prev = flat_prefix[state_size:].reshape(key_local.shape)
    query_wide = query_feat.astype(jnp.float32)
    carried_num = jnp.einsum(
        "thd,hde->the", query_wide, state_prev, precision=lax.Precision.HIGHEST
    )
    carried_den = jnp.einsum("thd,hd->th", query_wide, key_prev, precision=lax.Precision.HIGHEST)
    result = (local_num + carried_num) / (local_den.T + carried_den)[..., None]
    return result.astype(jnp.bfloat16).reshape(token_count, heads_here * HEAD_DIM)


def solution(mesh):
    return jax.shard_map(
        per_device,
        mesh=mesh,
        in_specs=(
            P("wide", "narrow", None, None),
            P(None, "wide"),
            P(None, "wide"),
            P(None, "wide"),
            P(None, None, "narrow"),
        ),
        out_specs=P("wide", "narrow"),
        check_vma=False,
    )
```
